256 devices in a mesh: pipe: 8 (over x, core), seq: 8 (over z), tp: 4 (over y).
Axes of the slice: x: 4, y: 4, z: 8, core: 2. Of those that a mesh axis runs over, the one named last changes fastest.
Arguments:
- query_fwd: bfloat16 [8, 4096, 32, 128], P('pipe', ('seq', 'tp')), may hold values from -60 to 60
- key_fwd: bfloat16 [8, 4096, 32, 128], P('pipe', ('seq', 'tp')), may hold values from -6 to 6
- value_fwd: bfloat16 [8, 4096, 32, 128], P('pipe', ('seq', 'tp')), may hold values from -18 to 18
- query_bwd: bfloat16 [8, 4096, 32, 128], P('pipe', ('seq', 'tp')), may hold values from -60 to 60
- key_bwd: bfloat16 [8, 4096, 32, 128], P('pipe', ('seq', 'tp')), may hold values from -6 to 6
- value_bwd: bfloat16 [8, 4096, 32, 128], P('pipe', ('seq', 'tp')), may hold values from -18 to 18
- grad_mix: bfloat16 [8, 4096, 32, 128], P('pipe', ('seq', 'tp')), may hold values from -24 to 24
- global_blocks: int32 [8, 32, 2], P('pipe', ('seq', 'tp')), may hold values from 0 to 63
- window: int32 [8, 32], P('pipe', ('seq', 'tp')), may hold values from 0 to 1, as said below
- rand_count: int32 [8, 32], P('pipe', ('seq', 'tp')), may hold values from 0 to 3, as said below
- rand_blocks: int32 [8, 32, 64, 3], P('pipe', ('seq', 'tp')), may hold values from 0 to 63
Outputs:
- next_input: bfloat16 [8, 4096, 32, 128], P('pipe', ('seq', 'tp'))
- input_grads: bfloat16 [3, 8, 4096, 32, 128], P(None, 'pipe', ('seq', 'tp'))
The draws below stay inside these ranges and needn't reach their ends.
Inputs may be any that keep to these rules, and one draw needn't show every extreme that they name: `window`: in every section some head has the half-width 1. `rand_count`: in every section some head has 3 random blocks; most heads have fewer.
All inputs are finite; a program needn't handle non-finite values.
Results may differ from the reference program's by a relative error of at most 0.0085.
Values may be sent and summed in bfloat16 or wider, within the bound.
No kernel may reach another device: no remote copies, remote signals or barrier semaphores. Data moves between devices by JAX's collectives and lax.ppermute only.
A program may use at most 192 MiB of HBM per device.

```python
import jax
import jax.numpy as jnp
from jax import lax

HDIM = 128
HEADS = 32
BLK = 64
GLOBAL = 2
WMAX = 1
R_MOST = 3
SEQ_LEN = 4096
NBLK = 64
SECTIONS = 8
SLOTS = 8


def normal_pair(key):
    shape = (SECTIONS, SEQ_LEN, HEADS, HDIM)
    queries = 2.0 * jax.random.truncated_normal(jax.random.fold_in(key, 11), -6.0, 6.0, shape, jnp.float32)
    keys = jax.random.truncated_normal(jax.random.fold_in(key, 12), -6.0, 6.0, shape, jnp.float32)
    return (queries, keys)


def query_key(key, micro):
    pair_key = jax.random.fold_in(key, 40 + micro)
    return normal_pair(pair_key)


def draw_query_fwd(key, part):
    return query_key(key, 1)[0].astype(jnp.bfloat16)


def draw_key_fwd(key, part):
    return query_key(key, 1)[1].astype(jnp.bfloat16)


def draw_query_bwd(key, part):
    return query_key(key, 2)[0].astype(jnp.bfloat16)


def draw_key_bwd(key, part):
    return query_key(key, 2)[1].astype(jnp.bfloat16)


def draw_window(key, part):
    key = jax.random.fold_in(key, 3)
    widths = jax.random.randint(jax.random.fold_in(key, 1), (SECTIONS, HEADS), 0, WMAX + 1)
    widest = jax.random.randint(jax.random.fold_in(key, 2), (SECTIONS,), 0, HEADS)
    heads = jnp.arange(HEADS)[None, :]
    return jnp.where(heads == widest[:, None], WMAX, widths).astype(jnp.int32)


def draw_rand_count(key, part):
    key = jax.random.fold_in(key, 5)
    first = jax.random.randint(jax.random.fold_in(key, 1), (SECTIONS, HEADS), 0, R_MOST + 1)
    second = jax.random.randint(jax.random.fold_in(key, 2), (SECTIONS, HEADS), 0, R_MOST + 1)
    busiest = jax.random.randint(jax.random.fold_in(key, 3), (SECTIONS,), 0, HEADS)
    heads = jnp.arange(HEADS)[None, :]
    return jnp.where(heads == busiest[:, None], R_MOST, jnp.minimum(first, second)).astype(jnp.int32)


def plant(result, stream_key, smallest, top_value):
    place = [jax.random.randint(jax.random.fold_in(stream_key, axis), (), 0, length) for axis, length in enumerate(result.shape)]
    longest = result.shape.index(max(result.shape))
    next_to = place[:longest] + [(place[longest] + 1) % result.shape[longest]] + place[longest + 1:]
    return result.at[tuple(place)].set(smallest).at[tuple(next_to)].set(top_value)


def block_levels(key, dims, shards, low, top_value):
    def one(position, parts):
        draws = jax.random.uniform(jax.random.fold_in(jax.random.fold_in(key, 6), position), (parts,), jnp.float32, low / len(shards), top_value / len(shards))
        return jnp.repeat(jnp.exp(draws), dims[position] // parts).reshape((-1,) + (1,) * (len(dims) - position - 1))

    level = one(*shards[0])
    for cut in shards[1:]:
        level = level * one(*cut)
    return level


def noise(own_key, shape, scale, bound, pieces=(), kind=jnp.bfloat16):
    values = jax.random.normal(own_key, shape, jnp.float32) * scale
    if len(pieces) > 0:
        values = block_levels(own_key, shape, pieces, -0.22, 0.18) * values
    return jnp.clip(values, min=-bound, max=bound).astype(kind)


def setup_inputs(seed: int = 0) -> dict:
    splits = jax.random.split(jax.random.key(seed), 12)
    return {
        "query_fwd": draw_query_fwd(jax.random.fold_in(splits[11], 71), 0),
        "key_fwd": draw_key_fwd(jax.random.fold_in(splits[11], 71), 0),
        "value_fwd": noise(splits[2], (SECTIONS, SEQ_LEN, HEADS, HDIM), 3.0, 18.0, ((0, 8), (1, 32))),
        "query_bwd": draw_query_bwd(jax.random.fold_in(splits[11], 71), 0),
        "key_bwd": draw_key_bwd(jax.random.fold_in(splits[11], 71), 0),
        "value_bwd": noise(splits[5], (SECTIONS, SEQ_LEN, HEADS, HDIM), 3.0, 18.0, ((0, 8), (1, 32))),
        "grad_mix": noise(splits[6], (SECTIONS, SEQ_LEN, HEADS, HDIM), 4.0, 24.0, ((0, 8), (1, 32))),
        "global_blocks": plant(jax.random.randint(splits[7], (SECTIONS, HEADS, GLOBAL), 0, NBLK), jax.random.fold_in(splits[7], 1), 0, NBLK - 1).astype(jnp.int32),
        "window": draw_window(jax.random.fold_in(splits[11], 71), 0),
        "rand_count": draw_rand_count(jax.random.fold_in(splits[11], 71), 0),
        "rand_blocks": plant(jax.random.randint(splits[10], (SECTIONS, HEADS, NBLK, R_MOST), 0, NBLK), jax.random.fold_in(splits[10], 1), 0, NBLK - 1).astype(jnp.int32),
    }


def key_slots(glob, win, count, rand_ids):
    blocks = jnp.arange(NBLK, dtype=jnp.int32)[:, None]
    glob_ids = jnp.broadcast_to(glob.astype(jnp.int32)[None, :], (NBLK, GLOBAL))
    glob_open = jnp.ones((NBLK, GLOBAL), jnp.bool_)
    offsets = jnp.arange(-WMAX, WMAX + 1, dtype=jnp.int32)[None, :]
    near = blocks + offsets
    near_open = (jnp.abs(offsets) <= win) & (near >= 0) & (near < NBLK)
    near = jnp.clip(near, 0, NBLK - 1).astype(jnp.int32)
    rand_open = jnp.broadcast_to(jnp.arange(R_MOST, dtype=jnp.int32)[None, :] < count, (NBLK, R_MOST))
    ids = jnp.concatenate([glob_ids, near, rand_ids.astype(jnp.int32)], axis=1)
    opened = jnp.concatenate([glob_open, near_open, rand_open], axis=1)
    same = ids[:, :, None] == ids[:, None, :]
    earlier = jnp.arange(SLOTS)[None, :] < jnp.arange(SLOTS)[:, None]
    repeated = jnp.any(same & opened[:, None, :] & earlier[None], axis=2)
    return ids, opened & jnp.logical_not(repeated)


def attend(queries, keys, values, ids, opened):
    qblk = queries.reshape(NBLK, BLK, HDIM).astype(jnp.float32)
    kblk = keys.reshape(NBLK, BLK, HDIM)[ids].reshape(NBLK, SLOTS * BLK, HDIM).astype(jnp.float32)
    vblk = values.reshape(NBLK, BLK, HDIM)[ids].reshape(NBLK, SLOTS * BLK, HDIM).astype(jnp.float32)
    open_keys = jnp.repeat(opened, BLK, axis=1)[:, None, :]
    scores = jnp.einsum("nqd,nkd->nqk", qblk, kblk) * (HDIM ** -0.5)
    scores = jnp.where(open_keys, scores, -1e30)
    top = jnp.max(scores, axis=-1, keepdims=True)
    weights = jnp.exp(scores - top)
    prob = weights / jnp.sum(weights, axis=-1, keepdims=True)
    prob_b = lax.optimization_barrier(prob.astype(jnp.bfloat16)).astype(jnp.float32)
    mixed = jnp.einsum("nqk,nkd->nqd", prob_b, vblk)
    return qblk, kblk, vblk, prob, prob_b, mixed


def backward(queries, keys, values, grad, ids, opened):
    qblk, kblk, vblk, prob, prob_b, mixed = attend(queries, keys, values, ids, opened)
    gblk = grad.reshape(NBLK, BLK, HDIM).astype(jnp.float32)
    delta = jnp.sum(gblk * mixed, axis=-1, keepdims=True)
    dprob = jnp.einsum("nqd,nkd->nqk", gblk, vblk)
    dscore = (prob * (dprob - delta) * (HDIM ** -0.5)).astype(jnp.bfloat16)
    dscore = lax.optimization_barrier(dscore).astype(jnp.float32)
    grad_q = jnp.einsum("nqk,nkd->nqd", dscore, kblk)
    key_part = jnp.einsum("nqk,nqd->nkd", dscore, qblk).reshape(NBLK, SLOTS, BLK, HDIM)
    value_part = jnp.einsum("nqk,nqd->nkd", prob_b, gblk).reshape(NBLK, SLOTS, BLK, HDIM)
    grad_k = jnp.zeros((NBLK, BLK, HDIM), jnp.float32).at[ids].add(key_part)
    grad_v = jnp.zeros((NBLK, BLK, HDIM), jnp.float32).at[ids].add(value_part)
    shape = (SEQ_LEN, HDIM)
    return (grad_q.reshape(shape).astype(jnp.bfloat16), grad_k.reshape(shape).astype(jnp.bfloat16),
            grad_v.reshape(shape).astype(jnp.bfloat16))


def heads_lead(tensor):
    return jnp.moveaxis(tensor, 1, 0)


def reference(query_fwd, key_fwd, value_fwd, query_bwd, key_bwd, value_bwd, grad_mix, global_blocks, window, rand_count, rand_blocks):
    def section(inputs):
        qf, kf, vf, qb, kb, vb, gm, globs, wins, counts, rids = inputs

        def head(items):
            aq, ak, av, bq, bk, bv, bg, glob, width, count, rand_ids = items
            ids, opened = key_slots(glob, width, count, rand_ids)
            mixed = attend(aq, ak, av, ids, opened)[5].reshape(SEQ_LEN, HDIM).astype(jnp.bfloat16)
            return mixed, backward(bq, bk, bv, bg, ids, opened)

        return lax.map(head, (heads_lead(qf), heads_lead(kf), heads_lead(vf), heads_lead(qb), heads_lead(kb),
                              heads_lead(vb), heads_lead(gm), globs, wins, counts, rids))

    mixed, grads = lax.map(section, (query_fwd, key_fwd, value_fwd, query_bwd, key_bwd, value_bwd, grad_mix,
                                   global_blocks, window, rand_count, rand_blocks))
    mixed = jnp.moveaxis(mixed, 1, 2)
    grads = jnp.moveaxis(jnp.stack(grads), 2, 3)
    next_input = jnp.concatenate([jnp.zeros_like(mixed[:1]), mixed[:-1]], axis=0)
    input_grads = jnp.concatenate([grads[:, 1:], jnp.zeros_like(grads[:, :1])], axis=1)
    return next_input, input_grads
```

```python
import math

import jax
import jax.numpy as jnp
from jax import lax
from jax.experimental import pallas as pl
from jax.experimental.pallas import tpu as pltpu
from jax.sharding import PartitionSpec as P

BLK = 64
GLOBAL = 2
WMAX = 1
R_MOST = 3
SLOTS = 8
HDIM = 128
SCALE = HDIM ** (-0.5)
LOG2E = math.log2(math.e)
MIB = 1 << 20


def passed_along(value, axis, steps):
    count = lax.axis_size(axis)
    first, last = (max(0, -steps), min(count, count - steps))
    return lax.ppermute(value, axis, [(source, source + steps) for source in range(first, last)])


def key_slots(glob, win, count, rand_ids):
    nblk = rand_ids.shape[0]
    blocks = jnp.arange(nblk, dtype=jnp.int32)[:, None]
    glob_ids = jnp.broadcast_to(glob[None, :], (nblk, GLOBAL))
    glob_open = jnp.ones((nblk, GLOBAL), jnp.bool_)
    offsets = jnp.arange(-WMAX, WMAX + 1, dtype=jnp.int32)[None, :]
    near = blocks + offsets
    near_open = (jnp.abs(offsets) <= win) & (near >= 0) & (near < nblk)
    near = jnp.clip(near, 0, nblk - 1)
    rand_open = jnp.broadcast_to(
        jnp.arange(R_MOST, dtype=jnp.int32)[None, :] < count, (nblk, R_MOST)
    )
    ids = jnp.concatenate([glob_ids, near, rand_ids], axis=1)
    opened = jnp.concatenate([glob_open, near_open, rand_open], axis=1)
    same = ids[:, :, None] == ids[:, None, :]
    earlier = jnp.arange(SLOTS)[None, :] < jnp.arange(SLOTS)[:, None]
    repeated = jnp.any(same & opened[:, None, :] & earlier[None], axis=2)
    return (ids, opened & jnp.logical_not(repeated))


def pack_kernel(count, *refs):
    ins, out, wide = refs[:count], refs[count], refs[count + 1]
    rows, heads, hdim = ins[0].shape
    for a, x in enumerate(ins):
        wide[a % 2] = x[...].reshape(rows * heads, hdim).astype(jnp.float32)
        for h in range(heads):
            out[h, a] = wide[a % 2, pl.ds(h, rows, stride=heads), :].astype(jnp.bfloat16)


def pack(arrays):
    rows, heads, hdim = arrays[0].shape
    count = len(arrays)
    return pl.pallas_call(
        lambda *refs: pack_kernel(count, *refs),
        out_shape=jax.ShapeDtypeStruct((heads, count, rows, hdim), jnp.bfloat16),
        scratch_shapes=[pltpu.VMEM((2, rows * heads, hdim), jnp.float32)],
        compiler_params=pltpu.CompilerParams(vmem_limit_bytes=40 * MIB),
        name="pack",
    )(*arrays)


def unpack_kernel(x, out, wide):
    heads, count, rows, hdim = x.shape
    for a in range(count):
        for h in range(heads):
            wide[a % 2, pl.ds(h, rows, stride=heads), :] = x[h, a].astype(jnp.float32)
        out[a] = wide[a % 2].astype(jnp.bfloat16).reshape(rows, heads, hdim)


def unpack(x):
    heads, count, rows, hdim = x.shape
    return pl.pallas_call(
        unpack_kernel,
        out_shape=jax.ShapeDtypeStruct((count, rows, heads, hdim), jnp.bfloat16),
        scratch_shapes=[pltpu.VMEM((2, rows * heads, hdim), jnp.float32)],
        compiler_params=pltpu.CompilerParams(vmem_limit_bytes=40 * MIB),
        name="unpack",
    )(x)


def dot(a, b, dims):
    return lax.dot_general(a, b, (dims, ((), ())), preferred_element_type=jnp.float32)


def block(ref, a, b):
    per = ref.shape[2] // BLK
    return ref[b // per, a, pl.ds(pl.multiple_of((b % per) * BLK, BLK), BLK), :]


def probabilities(q, keys, bias):
    scores = dot(q, keys, ((1,), (1,))) * (SCALE * LOG2E) + bias
    weights = jnp.exp2(scores - jnp.max(scores, axis=-1, keepdims=True))
    return weights * (1.0 / jnp.sum(weights, axis=-1, keepdims=True))


def forward_kernel(ids, bias, x, out):
    parts, _, rows, _ = x.shape
    per = rows // BLK

    def step(j, carry):
        for half in range(per):
            i = j * per + half
            picks = [ids[i, c] for c in range(SLOTS)]
            keys = jnp.concatenate([block(x, 1, b) for b in picks], axis=0)
            values = jnp.concatenate([block(x, 2, b) for b in picks], axis=0)
            q = x[j, 0, half * BLK : (half + 1) * BLK, :]
            prob = probabilities(q, keys, bias[pl.ds(i, 1), :]).astype(jnp.bfloat16)
            mixed = dot(prob, values, ((1,), (0,)))
            out[j, 0, half * BLK : (half + 1) * BLK, :] = mixed.astype(jnp.bfloat16)
        return carry

    lax.fori_loop(0, parts, step, 0)


def backward_kernel(ids, bias, x, out, dk, dv):
    parts, _, rows, _ = x.shape
    per = rows // BLK
    dk[...] = jnp.zeros_like(dk)
    dv[...] = jnp.zeros_like(dv)

    def step(j, carry):
        for half in range(per):
            i = j * per + half
            own = slice(half * BLK, (half + 1) * BLK)
            picks = [ids[i, c] for c in range(SLOTS)]
            keys = jnp.concatenate([block(x, 1, b) for b in picks], axis=0)
            values = jnp.concatenate([block(x, 2, b) for b in picks], axis=0)
            q = x[j, 0, own, :]
            g = x[j, 3, own, :]
            prob = probabilities(q, keys, bias[pl.ds(i, 1), :])
            prob_b = prob.astype(jnp.bfloat16)
            dprob = dot(g, values, ((1,), (1,)))
            delta = jnp.sum(prob_b.astype(jnp.float32) * dprob, axis=-1, keepdims=True)
            dscore = (prob * ((dprob - delta) * SCALE)).astype(jnp.bfloat16)
            out[j, 0, own, :] = dot(dscore, keys, ((1,), (0,))).astype(jnp.bfloat16)
            key_part = dot(dscore, q, ((0,), (0,)))
            value_part = dot(prob_b, g, ((0,), (0,)))
            for c, b in enumerate(picks):
                at = pl.ds(pl.multiple_of(b * BLK, BLK), BLK)
                dk[at, :] += key_part[c * BLK : (c + 1) * BLK]
                dv[at, :] += value_part[c * BLK : (c + 1) * BLK]
        return carry

    lax.fori_loop(0, parts, step, 0)
    hdim = x.shape[3]
    out[:, 1] = dk[...].reshape(parts, rows, hdim).astype(jnp.bfloat16)
    out[:, 2] = dv[...].reshape(parts, rows, hdim).astype(jnp.bfloat16)


def attention(kernel, results, x, ids, bias, scratch, cost):
    parts, _, rows, hdim = x.shape
    return pl.pallas_call(
        kernel,
        out_shape=jax.ShapeDtypeStruct((parts, results, rows, hdim), jnp.bfloat16),
        in_specs=[
            pl.BlockSpec(memory_space=pltpu.SMEM),
            pl.BlockSpec(memory_space=pltpu.VMEM),
            pl.BlockSpec(memory_space=pltpu.VMEM),
        ],
        scratch_shapes=scratch,
        compiler_params=pltpu.CompilerParams(vmem_limit_bytes=40 * MIB),
        cost_estimate=cost,
        name=kernel.__name__,
    )(ids, bias, x)


def exchange(x):
    return lax.all_to_all(x, ("seq", "tp"), split_axis=0, concat_axis=0, tiled=True)


def slots_and_bias(glob, win, count, rand_ids):
    ids, opened = key_slots(glob, win, count, rand_ids)
    bias = jnp.where(jnp.repeat(opened, BLK, axis=1), 0.0, -1e30).astype(jnp.float32)
    return ids, bias


def body(
    query_fwd,
    key_fwd,
    value_fwd,
    query_bwd,
    key_bwd,
    value_bwd,
    grad_mix,
    global_blocks,
    window,
    rand_count,
    rand_blocks,
):
    ids, bias = slots_and_bias(
        global_blocks[0, 0], window[0, 0], rand_count[0, 0], rand_blocks[0, 0]
    )
    bwd = exchange(pack((query_bwd[0], key_bwd[0], value_bwd[0], grad_mix[0])))
    fwd = exchange(pack((query_fwd[0], key_fwd[0], value_fwd[0])))
    tokens = bwd.shape[0] * bwd.shape[2]
    work = tokens * SLOTS * BLK * HDIM * 2
    grads = attention(
        backward_kernel, 3, bwd, ids, bias,
        [pltpu.VMEM((tokens, HDIM), jnp.float32)] * 2,
        pl.CostEstimate(flops=5 * work * 4, bytes_accessed=8 * MIB, transcendentals=0),
    )
    grads = exchange(passed_along(grads, "pipe", -1))
    mixed = attention(
        forward_kernel, 1, fwd, ids, bias, [],
        pl.CostEstimate(flops=2 * work * 4, bytes_accessed=4 * MIB, transcendentals=0),
    )
    mixed = exchange(passed_along(mixed, "pipe", 1))
    return (unpack(mixed), unpack(grads)[:, None])


def solution(mesh):
    rows = P("pipe", ("seq", "tp"), None, None)
    placed = (rows,) * 7 + (
        P("pipe", ("seq", "tp"), None),
        P("pipe", ("seq", "tp")),
        P("pipe", ("seq", "tp")),
        P("pipe", ("seq", "tp"), None, None),
    )
    return jax.shard_map(
        body,
        mesh=mesh,
        in_specs=placed,
        out_specs=(rows, P(None, "pipe", ("seq", "tp"), None, None)),
        check_vma=False,
    )
```

```python
import math

import jax
import jax.numpy as jnp
from jax import lax
from jax.experimental import pallas as pl
from jax.experimental.pallas import tpu as pltpu
from jax.sharding import PartitionSpec as P

BLK = 64
GLOBAL = 2
WMAX = 1
R_MOST = 3
SLOTS = 8
HDIM = 128
SCALE = HDIM ** (-0.5)
LOG2E = math.log2(math.e)
MIB = 1 << 20
STEP = 8


def passed_along(value, axis, steps):
    count = lax.axis_size(axis)
    first, last = (max(0, -steps), min(count, count - steps))
    return lax.ppermute(value, axis, [(source, source + steps) for source in range(first, last)])


def key_slots(glob, win, count, rand_ids):
    nblk = rand_ids.shape[0]
    blocks = jnp.arange(nblk, dtype=jnp.int32)[:, None]
    glob_ids = jnp.broadcast_to(glob[None, :], (nblk, GLOBAL))
    glob_open = jnp.ones((nblk, GLOBAL), jnp.bool_)
    offsets = jnp.arange(-WMAX, WMAX + 1, dtype=jnp.int32)[None, :]
    near = blocks + offsets
    near_open = (jnp.abs(offsets) <= win) & (near >= 0) & (near < nblk)
    near = jnp.clip(near, 0, nblk - 1)
    rand_open = jnp.broadcast_to(
        jnp.arange(R_MOST, dtype=jnp.int32)[None, :] < count, (nblk, R_MOST)
    )
    ids = jnp.concatenate([glob_ids, near, rand_ids], axis=1)
    opened = jnp.concatenate([glob_open, near_open, rand_open], axis=1)
    same = ids[:, :, None] == ids[:, None, :]
    earlier = jnp.arange(SLOTS)[None, :] < jnp.arange(SLOTS)[:, None]
    repeated = jnp.any(same & opened[:, None, :] & earlier[None], axis=2)
    return (ids, opened & jnp.logical_not(repeated))


def pack_kernel(count, *refs):
    for a in range(count):
        refs[count][:, a] = jnp.swapaxes(refs[a][...], 0, 1)


def pack(arrays):
    rows, heads, hdim = arrays[0].shape
    count = len(arrays)
    chunk = rows // 2
    return pl.pallas_call(
        lambda *refs: pack_kernel(count, *refs),
        grid=(rows // chunk,),
        in_specs=[pl.BlockSpec((chunk, heads, hdim), lambda i: (i, 0, 0))] * count,
        out_specs=pl.BlockSpec((heads, count, chunk, hdim), lambda i: (0, 0, i, 0)),
        out_shape=jax.ShapeDtypeStruct((heads, count, rows, hdim), jnp.bfloat16),
        compiler_params=pltpu.CompilerParams(vmem_limit_bytes=60 * MIB),
        cost_estimate=pl.CostEstimate(
            flops=0, bytes_accessed=4 * count * rows * heads * hdim, transcendentals=0
        ),
        name="pack",
    )(*arrays)


def unpack_kernel(x, out):
    for a in range(x.shape[1]):
        out[a] = jnp.swapaxes(x[:, a], 0, 1)


def unpack(x):
    heads, count, rows, hdim = x.shape
    chunk = rows // 2
    return pl.pallas_call(
        unpack_kernel,
        grid=(rows // chunk,),
        in_specs=[pl.BlockSpec((heads, count, chunk, hdim), lambda i: (0, 0, i, 0))],
        out_specs=pl.BlockSpec((count, chunk, heads, hdim), lambda i: (0, i, 0, 0)),
        out_shape=jax.ShapeDtypeStruct((count, rows, heads, hdim), jnp.bfloat16),
        compiler_params=pltpu.CompilerParams(vmem_limit_bytes=60 * MIB),
        cost_estimate=pl.CostEstimate(
            flops=0, bytes_accessed=4 * count * rows * heads * hdim, transcendentals=0
        ),
        name="unpack",
    )(x)


def tie_kernel(x, first, out):
    del x, first, out


def after(x, first):
    anywhere = pl.BlockSpec(memory_space=pl.ANY)
    return pl.pallas_call(
        tie_kernel,
        in_specs=[anywhere, anywhere],
        out_specs=anywhere,
        out_shape=jax.ShapeDtypeStruct(x.shape, x.dtype),
        input_output_aliases={0: 0},
        name="after",
    )(x, first)


def dot(a, b, dims):
    return lax.dot_general(a, b, (dims, ((), ())), preferred_element_type=jnp.float32)


def block(ref, a, b):
    per = ref.shape[2] // BLK
    return ref[b // per, a, pl.ds(pl.multiple_of((b % per) * BLK, BLK), BLK), :]


def gather(x, a, picks):
    return jnp.concatenate([block(x, a, b) for b in picks], axis=0)


def probabilities(scores, bias):
    scores = [s * (SCALE * LOG2E) + b for s, b in zip(scores, bias)]
    weights = [jnp.exp2(s - jnp.max(s, axis=-1, keepdims=True)) for s in scores]
    return [w * (1.0 / jnp.sum(w, axis=-1, keepdims=True)) for w in weights]


def step_blocks(t, ids, x):
    per = x.shape[2] // BLK
    blocks = [t * STEP + n for n in range(STEP)]
    picks = [[ids[i, c] for c in range(SLOTS)] for i in blocks]
    places = [
        (t * (STEP // per) + n // per, slice((n % per) * BLK, (n % per + 1) * BLK))
        for n in range(STEP)
    ]
    return blocks, picks, places


def forward_kernel(ids, bias, x, first, out):
    del first

    def step(t, carry):
        blocks, picks, places = step_blocks(t, ids, x)
        keys = [gather(x, 1, p) for p in picks]
        values = [gather(x, 2, p) for p in picks]
        queries = [x[j, 0, own, :] for j, own in places]
        scores = [dot(q, k, ((1,), (1,))) for q, k in zip(queries, keys)]
        prob = probabilities(scores, [bias[pl.ds(i, 1), :] for i in blocks])
        prob = [p.astype(jnp.bfloat16) for p in prob]
        for (j, own), p, v in zip(places, prob, values):
            out[j, 0, own, :] = dot(p, v, ((1,), (0,))).astype(jnp.bfloat16)
        return carry

    lax.fori_loop(0, ids.shape[0] // STEP, step, 0)


def backward_kernel(ids, bias, x, out, dk, dv):
    parts, _, rows, hdim = x.shape
    dk[...] = jnp.zeros_like(dk)
    dv[...] = jnp.zeros_like(dv)

    def step(t, carry):
        blocks, picks, places = step_blocks(t, ids, x)
        keys = [gather(x, 1, p) for p in picks]
        values = [gather(x, 2, p) for p in picks]
        queries = [x[j, 0, own, :] for j, own in places]
        grads = [x[j, 3, own, :] for j, own in places]
        scores = [dot(q, k, ((1,), (1,))) for q, k in zip(queries, keys)]
        dprob = [dot(g, v, ((1,), (1,))) for g, v in zip(grads, values)]
        prob = probabilities(scores, [bias[pl.ds(i, 1), :] for i in blocks])
        prob_b = [p.astype(jnp.bfloat16) for p in prob]
        value_part = [dot(p, g, ((0,), (0,))) for p, g in zip(prob_b, grads)]
        delta = [
            jnp.sum(p.astype(jnp.float32) * d, axis=-1, keepdims=True)
            for p, d in zip(prob_b, dprob)
        ]
        dscore = [
            (p * ((d - e) * SCALE)).astype(jnp.bfloat16) for p, d, e in zip(prob, dprob, delta)
        ]
        key_part = [dot(d, q, ((0,), (0,))) for d, q in zip(dscore, queries)]
        for (j, own), d, k in zip(places, dscore, keys):
            out[j, 0, own, :] = dot(d, k, ((1,), (0,))).astype(jnp.bfloat16)
        for pick, kp, vp in zip(picks, key_part, value_part):
            for c, b in enumerate(pick):
                at = pl.ds(pl.multiple_of(b * BLK, BLK), BLK)
                dk[at, :] += kp[c * BLK : (c + 1) * BLK]
                dv[at, :] += vp[c * BLK : (c + 1) * BLK]
        return carry

    lax.fori_loop(0, ids.shape[0] // STEP, step, 0)
    out[:, 1] = dk[...].reshape(parts, rows, hdim).astype(jnp.bfloat16)
    out[:, 2] = dv[...].reshape(parts, rows, hdim).astype(jnp.bfloat16)


def attention(kernel, results, ids, bias, x, rest, scratch, matmuls):
    parts, _, rows, hdim = x.shape
    work = parts * rows * SLOTS * BLK * hdim * 2
    return pl.pallas_call(
        kernel,
        out_shape=jax.ShapeDtypeStruct((parts, results, rows, hdim), jnp.bfloat16),
        in_specs=[
            pl.BlockSpec(memory_space=pltpu.SMEM),
            pl.BlockSpec(memory_space=pltpu.VMEM),
            pl.BlockSpec(memory_space=pltpu.VMEM),
        ]
        + [pl.BlockSpec(memory_space=pl.ANY)] * len(rest),
        scratch_shapes=scratch,
        compiler_params=pltpu.CompilerParams(vmem_limit_bytes=40 * MIB),
        cost_estimate=pl.CostEstimate(
            flops=4 * matmuls * work, bytes_accessed=8 * MIB, transcendentals=0
        ),
        name=kernel.__name__,
    )(ids, bias, x, *rest)


def exchange(x):
    return lax.all_to_all(x, ("seq", "tp"), split_axis=0, concat_axis=0, tiled=True)


def slots_and_bias(glob, win, count, rand_ids):
    ids, opened = key_slots(glob, win, count, rand_ids)
    bias = jnp.where(jnp.repeat(opened, BLK, axis=1), 0.0, -1e30).astype(jnp.float32)
    return ids, bias


def body(
    query_fwd,
    key_fwd,
    value_fwd,
    query_bwd,
    key_bwd,
    value_bwd,
    grad_mix,
    global_blocks,
    window,
    rand_count,
    rand_blocks,
):
    ids, bias = slots_and_bias(
        global_blocks[0, 0], window[0, 0], rand_count[0, 0], rand_blocks[0, 0]
    )
    bwd = exchange(pack((query_bwd[0], key_bwd[0], value_bwd[0], grad_mix[0])))
    fwd = pack((query_fwd[0], key_fwd[0], value_fwd[0]))
    fwd, ids, bias = lax.optimization_barrier((fwd, ids, bias))
    fwd = exchange(fwd)
    tokens = bwd.shape[0] * bwd.shape[2]
    grads = attention(
        backward_kernel, 3, ids, bias, bwd, [], [pltpu.VMEM((tokens, HDIM), jnp.float32)] * 2, 5
    )
    grads = passed_along(grads, "pipe", -1)
    mixed = attention(forward_kernel, 1, ids, bias, fwd, [grads], [], 2)
    mixed = passed_along(mixed, "pipe", 1)
    grads = exchange(grads)
    mixed = exchange(after(mixed, grads))
    return (unpack(mixed), unpack(grads)[:, None])


def solution(mesh):
    rows = P("pipe", ("seq", "tp"), None, None)
    placed = (rows,) * 7 + (
        P("pipe", ("seq", "tp"), None),
        P("pipe", ("seq", "tp")),
        P("pipe", ("seq", "tp")),
        P("pipe", ("seq", "tp"), None, None),
    )
    return jax.shard_map(
        body,
        mesh=mesh,
        in_specs=placed,
        out_specs=(rows, P(None, "pipe", ("seq", "tp"), None, None)),
        check_vma=False,
    )
```

```python
import math

import jax
import jax.numpy as jnp
from jax import lax
from jax.experimental import pallas as pl
from jax.experimental.pallas import tpu as pltpu
from jax.sharding import PartitionSpec as P

BLK = 64
GLOBAL = 2
WMAX = 1
R_MOST = 3
SLOTS = 8
HDIM = 128
SCALE = HDIM ** (-0.5)
LOG2E = math.log2(math.e)
MIB = 1 << 20
STEP = 8
QUARTERS = 4


def passed_along(value, axis, steps):
    count = lax.axis_size(axis)
    first, last = (max(0, -steps), min(count, count - steps))
    return lax.ppermute(value, axis, [(source, source + steps) for source in range(first, last)])


def key_slots(glob, win, count, rand_ids):
    nblk = rand_ids.shape[0]
    blocks = jnp.arange(nblk, dtype=jnp.int32)[:, None]
    glob_ids = jnp.broadcast_to(glob[None, :], (nblk, GLOBAL))
    glob_open = jnp.ones((nblk, GLOBAL), jnp.bool_)
    offsets = jnp.arange(-WMAX, WMAX + 1, dtype=jnp.int32)[None, :]
    near = blocks + offsets
    near_open = (jnp.abs(offsets) <= win) & (near >= 0) & (near < nblk)
    near = jnp.clip(near, 0, nblk - 1)
    rand_open = jnp.broadcast_to(
        jnp.arange(R_MOST, dtype=jnp.int32)[None, :] < count, (nblk, R_MOST)
    )
    ids = jnp.concatenate([glob_ids, near, rand_ids], axis=1)
    opened = jnp.concatenate([glob_open, near_open, rand_open], axis=1)
    same = ids[:, :, None] == ids[:, None, :]
    earlier = jnp.arange(SLOTS)[None, :] < jnp.arange(SLOTS)[:, None]
    repeated = jnp.any(same & opened[:, None, :] & earlier[None], axis=2)
    return (ids, opened & jnp.logical_not(repeated))


def pack_first_kernel(stage, *refs):
    back, front, out, (wide, sem) = refs[:4], refs[4:7], refs[7], refs[8:]
    rows = back[0].shape[0]
    chunks = sem.shape[1]
    size = rows // chunks

    def copy(x, a, c):
        at = pl.ds(c * size, size)
        return pltpu.make_async_copy(x.at[at], wide.at[a, at], sem.at[a, c])

    @pl.when(stage[0] != 0)
    def _():
        for c in range(chunks):
            for a in range(4):
                copy(back[a], a, c).start()

    @pl.when(stage[0] == 0)
    def _():
        for c in range(chunks):
            for a in range(4):
                copy(front[min(a, 2)], a, c).start()

    for c in range(chunks):
        for a in range(4):
            copy(back[a], a, c).wait()
            out[:, a, c * size : (c + 1) * size] = jnp.swapaxes(
                wide[a, c * size : (c + 1) * size], 0, 1
            )


def pack_first(stage, back, front):
    rows, heads, hdim = back[0].shape
    return pl.pallas_call(
        pack_first_kernel,
        in_specs=[pl.BlockSpec(memory_space=pltpu.SMEM)]
        + [pl.BlockSpec(memory_space=pl.ANY)] * 7,
        out_shape=jax.ShapeDtypeStruct((heads, 4, rows, hdim), jnp.bfloat16),
        scratch_shapes=[
            pltpu.VMEM((4, rows, heads, hdim), jnp.bfloat16),
            pltpu.SemaphoreType.DMA((4, 4)),
        ],
        compiler_params=pltpu.CompilerParams(vmem_limit_bytes=60 * MIB),
        name="pack_first",
    )(stage, *back, *front)


def pack_rest_kernel(*refs):
    ins, lead, rest = refs[:-2], refs[-2], refs[-1]
    quarter = ins[0].shape[0] // QUARTERS
    for a, x in enumerate(ins):
        heads = jnp.swapaxes(x[...], 0, 1)
        lead[:, a] = heads[:, :-quarter]
        rest[:, a] = heads[:, quarter:]


def pack_rest(arrays):
    rows, heads, hdim = arrays[0].shape
    shape = (heads, len(arrays), rows - rows // QUARTERS, hdim)
    return pl.pallas_call(
        pack_rest_kernel,
        out_shape=[jax.ShapeDtypeStruct(shape, jnp.bfloat16)] * 2,
        compiler_params=pltpu.CompilerParams(vmem_limit_bytes=60 * MIB),
        cost_estimate=pl.CostEstimate(flops=0, bytes_accessed=9 * MIB, transcendentals=0),
        name="pack_rest",
    )(*arrays)


def from_end(stage, stages):
    return jnp.minimum(stage, stages - 1 - stage)


def merge_kernel(stages, stage, received, rest, out):
    lent = QUARTERS - 1 - from_end(stage[0], stages)
    quarter = out.shape[2] // (QUARTERS - 1)
    for f in range(QUARTERS - 1):
        at = slice(f * quarter, (f + 1) * quarter)

        @pl.when(f < lent)
        def _():
            out[:, :, at] = received[:, :, at]

        @pl.when(f >= lent)
        def _():
            out[:, :, at] = rest[:, :, at]


def merge(stage, stages, received, rest):
    return pl.pallas_call(
        lambda *refs: merge_kernel(stages, *refs),
        in_specs=[pl.BlockSpec(memory_space=pltpu.SMEM)]
        + [pl.BlockSpec(memory_space=pltpu.VMEM)] * 2,
        out_shape=jax.ShapeDtypeStruct(rest.shape, rest.dtype),
        compiler_params=pltpu.CompilerParams(vmem_limit_bytes=40 * MIB),
        cost_estimate=pl.CostEstimate(flops=0, bytes_accessed=7 * MIB, transcendentals=0),
        name="merge",
    )(stage, received, rest)


def outward(stages):
    half = stages // 2
    return [(p, p - 1) for p in range(1, half)] + [(p, p + 1) for p in range(half, stages - 1)]


def unpack_kernel(x, out):
    for a in range(x.shape[1]):
        out[a] = jnp.swapaxes(x[:, a], 0, 1)


def unpack(x):
    heads, count, rows, hdim = x.shape
    chunk = rows // 2
    return pl.pallas_call(
        unpack_kernel,
        grid=(rows // chunk,),
        in_specs=[pl.BlockSpec((heads, count, chunk, hdim), lambda i: (0, 0, i, 0))],
        out_specs=pl.BlockSpec((count, chunk, heads, hdim), lambda i: (0, i, 0, 0)),
        out_shape=jax.ShapeDtypeStruct((count, rows, heads, hdim), jnp.bfloat16),
        compiler_params=pltpu.CompilerParams(vmem_limit_bytes=60 * MIB),
        cost_estimate=pl.CostEstimate(
            flops=0, bytes_accessed=4 * count * rows * heads * hdim, transcendentals=0
        ),
        name="unpack",
    )(x)


def tie_kernel(x, first, out):
    del x, first, out


def after(x, first):
    anywhere = pl.BlockSpec(memory_space=pl.ANY)
    return pl.pallas_call(
        tie_kernel,
        in_specs=[anywhere, anywhere],
        out_specs=anywhere,
        out_shape=jax.ShapeDtypeStruct(x.shape, x.dtype),
        input_output_aliases={0: 0},
        name="after",
    )(x, first)


def dot(a, b, dims):
    return lax.dot_general(a, b, (dims, ((), ())), preferred_element_type=jnp.float32)


def block(ref, a, b):
    per = ref.shape[2] // BLK
    return ref[b // per, a, pl.ds(pl.multiple_of((b % per) * BLK, BLK), BLK), :]


def gather(x, a, picks):
    return jnp.concatenate([block(x, a, b) for b in picks], axis=0)


def probabilities(scores, bias):
    scores = [s * (SCALE * LOG2E) + b for s, b in zip(scores, bias)]
    weights = [jnp.exp2(s - jnp.max(s, axis=-1, keepdims=True)) for s in scores]
    return [w * (1.0 / jnp.sum(w, axis=-1, keepdims=True)) for w in weights]


def step_blocks(t, ids, x):
    per = x.shape[2] // BLK
    blocks = [t * STEP + n for n in range(STEP)]
    picks = [[ids[i, c] for c in range(SLOTS)] for i in blocks]
    places = [
        (t * (STEP // per) + n // per, slice((n % per) * BLK, (n % per + 1) * BLK))
        for n in range(STEP)
    ]
    return blocks, picks, places


def forward_kernel(stages, stage, ids, bias, whole, own, back, first, out, x):
    del first
    edge = from_end(stage[0], stages)
    lent = QUARTERS - edge
    quarter = x.shape[2] // QUARTERS

    @pl.when(edge == 0)
    def _():
        x[...] = whole[:, :3]

    for e in range(QUARTERS):
        to = slice(e * quarter, (e + 1) * quarter)

        if e < QUARTERS - 1:

            @pl.when((edge > 0) & (e < lent))
            def _():
                x[:, :, to] = back[:, :, to]

        if e > 0:

            @pl.when((edge > 0) & (e >= lent))
            def _():
                x[:, :, to] = own[:, :, (e - 1) * quarter : e * quarter]

    def step(t, carry):
        blocks, picks, places = step_blocks(t, ids, x)
        keys = [gather(x, 1, p) for p in picks]
        values = [gather(x, 2, p) for p in picks]
        queries = [x[j, 0, own, :] for j, own in places]
        scores = [dot(q, k, ((1,), (1,))) for q, k in zip(queries, keys)]
        prob = probabilities(scores, [bias[pl.ds(i, 1), :] for i in blocks])
        prob = [p.astype(jnp.bfloat16) for p in prob]
        for (j, own), p, v in zip(places, prob, values):
            out[j, 0, own, :] = dot(p, v, ((1,), (0,))).astype(jnp.bfloat16)
        return carry

    lax.fori_loop(0, ids.shape[0] // STEP, step, 0)


def backward_kernel(stages, stage, ids, bias, x, out, dk, dv):
    del stages, stage
    parts, _, rows, hdim = x.shape
    dk[...] = jnp.zeros_like(dk)
    dv[...] = jnp.zeros_like(dv)

    def step(t, carry):
        blocks, picks, places = step_blocks(t, ids, x)
        keys = [gather(x, 1, p) for p in picks]
        values = [gather(x, 2, p) for p in picks]
        queries = [x[j, 0, own, :] for j, own in places]
        grads = [x[j, 3, own, :] for j, own in places]
        scores = [dot(q, k, ((1,), (1,))) for q, k in zip(queries, keys)]
        dprob = [dot(g, v, ((1,), (1,))) for g, v in zip(grads, values)]
        prob = probabilities(scores, [bias[pl.ds(i, 1), :] for i in blocks])
        prob_b = [p.astype(jnp.bfloat16) for p in prob]
        value_part = [dot(p, g, ((0,), (0,))) for p, g in zip(prob_b, grads)]
        delta = [
            jnp.sum(p.astype(jnp.float32) * d, axis=-1, keepdims=True)
            for p, d in zip(prob_b, dprob)
        ]
        dscore = [
            (p * ((d - e) * SCALE)).astype(jnp.bfloat16) for p, d, e in zip(prob, dprob, delta)
        ]
        key_part = [dot(d, q, ((0,), (0,))) for d, q in zip(dscore, queries)]
        for (j, own), d, k in zip(places, dscore, keys):
            out[j, 0, own, :] = dot(d, k, ((1,), (0,))).astype(jnp.bfloat16)
        for pick, kp, vp in zip(picks, key_part, value_part):
            for c, b in enumerate(pick):
                at = pl.ds(pl.multiple_of(b * BLK, BLK), BLK)
                dk[at, :] += kp[c * BLK : (c + 1) * BLK]
                dv[at, :] += vp[c * BLK : (c + 1) * BLK]
        return carry

    lax.fori_loop(0, ids.shape[0] // STEP, step, 0)
    out[:, 1] = dk[...].reshape(parts, rows, hdim).astype(jnp.bfloat16)
    out[:, 2] = dv[...].reshape(parts, rows, hdim).astype(jnp.bfloat16)


def attention(kernel, results, stage, ids, bias, ins, rest, scratch, matmuls):
    parts, _, rows, hdim = ins[0].shape
    work = parts * rows * SLOTS * BLK * hdim * 2
    stages = lax.axis_size("pipe")
    in_smem = pl.BlockSpec(memory_space=pltpu.SMEM)
    in_vmem = pl.BlockSpec(memory_space=pltpu.VMEM)
    return pl.pallas_call(
        lambda *refs: kernel(stages, *refs),
        out_shape=jax.ShapeDtypeStruct((parts, results, rows, hdim), jnp.bfloat16),
        in_specs=[in_smem, in_smem, in_vmem]
        + [in_vmem] * len(ins)
        + [pl.BlockSpec(memory_space=pl.ANY)] * len(rest),
        scratch_shapes=scratch,
        compiler_params=pltpu.CompilerParams(vmem_limit_bytes=40 * MIB),
        cost_estimate=pl.CostEstimate(
            flops=4 * matmuls * work, bytes_accessed=8 * MIB, transcendentals=0
        ),
        name=kernel.__name__,
    )(stage, ids, bias, *ins, *rest)


def exchange(x):
    return lax.all_to_all(x, ("seq", "tp"), split_axis=0, concat_axis=0, tiled=True)


def slots_and_bias(glob, win, count, rand_ids):
    ids, opened = key_slots(glob, win, count, rand_ids)
    bias = jnp.where(jnp.repeat(opened, BLK, axis=1), 0.0, -1e30).astype(jnp.float32)
    return ids, bias


def body(
    query_fwd,
    key_fwd,
    value_fwd,
    query_bwd,
    key_bwd,
    value_bwd,
    grad_mix,
    global_blocks,
    window,
    rand_count,
    rand_blocks,
):
    ids, bias = slots_and_bias(
        global_blocks[0, 0], window[0, 0], rand_count[0, 0], rand_blocks[0, 0]
    )
    stages = lax.axis_size("pipe")
    stage = lax.axis_index("pipe").astype(jnp.int32)[None]
    front = (query_fwd[0], key_fwd[0], value_fwd[0])
    first = exchange(
        pack_first(stage, (query_bwd[0], key_bwd[0], value_bwd[0], grad_mix[0]), front)
    )
    lead, rest = pack_rest(front)
    received = lax.ppermute(lead, "pipe", outward(stages))
    second = merge(stage, stages, received, rest)
    second, ids, bias = lax.optimization_barrier((second, ids, bias))
    second = exchange(second)
    tokens = first.shape[0] * first.shape[2]
    grads = attention(
        backward_kernel, 3, stage, ids, bias, [first], [],
        [pltpu.VMEM((tokens, HDIM), jnp.float32)] * 2, 5,
    )
    grads = passed_along(grads, "pipe", -1)
    back = lax.ppermute(second, "pipe", [(b, a) for a, b in outward(stages)])
    mixed = attention(
        forward_kernel, 1, stage, ids, bias, [first, second, back], [grads],
        [pltpu.VMEM((first.shape[0], 3) + first.shape[2:], jnp.bfloat16)], 2,
    )
    mixed = passed_along(mixed, "pipe", 1)
    grads = exchange(grads)
    mixed = exchange(after(mixed, grads))
    return (unpack(mixed), unpack(grads)[:, None])


def solution(mesh):
    rows = P("pipe", ("seq", "tp"), None, None)
    placed = (rows,) * 7 + (
        P("pipe", ("seq", "tp"), None),
        P("pipe", ("seq", "tp")),
        P("pipe", ("seq", "tp")),
        P("pipe", ("seq", "tp"), None, None),
    )
    return jax.shard_map(
        body,
        mesh=mesh,
        in_specs=placed,
        out_specs=(rows, P(None, "pipe", ("seq", "tp"), None, None)),
        check_vma=False,
    )
```

```python
import math

import jax
import jax.numpy as jnp
from jax import lax
from jax.experimental import pallas as pl
from jax.experimental.pallas import tpu as pltpu
from jax.sharding import PartitionSpec as P

BLK = 64
GLOBAL = 2
WMAX = 1
R_MOST = 3
SLOTS = 8
HDIM = 128
SCALE = HDIM ** (-0.5)
LOG2E = math.log2(math.e)
MIB = 1 << 20
STEP = 8
QUARTERS = 4
EIGHTHS = 8


def passed_along(value, axis, steps):
    count = lax.axis_size(axis)
    first, last = (max(0, -steps), min(count, count - steps))
    return lax.ppermute(value, axis, [(source, source + steps) for source in range(first, last)])


def key_slots(glob, win, count, rand_ids):
    nblk = rand_ids.shape[0]
    blocks = jnp.arange(nblk, dtype=jnp.int32)[:, None]
    glob_ids = jnp.broadcast_to(glob[None, :], (nblk, GLOBAL))
    glob_open = jnp.ones((nblk, GLOBAL), jnp.bool_)
    offsets = jnp.arange(-WMAX, WMAX + 1, dtype=jnp.int32)[None, :]
    near = blocks + offsets
    near_open = (jnp.abs(offsets) <= win) & (near >= 0) & (near < nblk)
    near = jnp.clip(near, 0, nblk - 1)
    rand_open = jnp.broadcast_to(
        jnp.arange(R_MOST, dtype=jnp.int32)[None, :] < count, (nblk, R_MOST)
    )
    ids = jnp.concatenate([glob_ids, near, rand_ids], axis=1)
    opened = jnp.concatenate([glob_open, near_open, rand_open], axis=1)
    same = ids[:, :, None] == ids[:, None, :]
    earlier = jnp.arange(SLOTS)[None, :] < jnp.arange(SLOTS)[:, None]
    repeated = jnp.any(same & opened[:, None, :] & earlier[None], axis=2)
    return (ids, opened & jnp.logical_not(repeated))


def pack_first_kernel(stage, *refs):
    back, front, out, (wide, sem) = refs[:4], refs[4:7], refs[7], refs[8:]
    rows = back[0].shape[0]
    chunks = sem.shape[1]
    size = rows // chunks

    def copy(x, a, c):
        at = pl.ds(c * size, size)
        return pltpu.make_async_copy(x.at[at], wide.at[a, at], sem.at[a, c])

    @pl.when(stage[0] != 0)
    def _():
        for c in range(chunks):
            for a in range(4):
                copy(back[a], a, c).start()

    @pl.when(stage[0] == 0)
    def _():
        for c in range(chunks):
            for a in range(4):
                copy(front[min(a, 2)], a, c).start()

    for c in range(chunks):
        for a in range(4):
            copy(back[a], a, c).wait()
            out[:, a, c * size : (c + 1) * size] = jnp.swapaxes(
                wide[a, c * size : (c + 1) * size], 0, 1
            )


def pack_first(stage, back, front):
    rows, heads, hdim = back[0].shape
    return pl.pallas_call(
        pack_first_kernel,
        in_specs=[pl.BlockSpec(memory_space=pltpu.SMEM)]
        + [pl.BlockSpec(memory_space=pl.ANY)] * 7,
        out_shape=jax.ShapeDtypeStruct((heads, 4, rows, hdim), jnp.bfloat16),
        scratch_shapes=[
            pltpu.VMEM((4, rows, heads, hdim), jnp.bfloat16),
            pltpu.SemaphoreType.DMA((4, 4)),
        ],
        compiler_params=pltpu.CompilerParams(vmem_limit_bytes=60 * MIB),
        name="pack_first",
    )(stage, *back, *front)


def pack_rest_kernel(*refs):
    ins, lead, rest = refs[:-2], refs[-2], refs[-1]
    quarter = ins[0].shape[0] // QUARTERS
    for a, x in enumerate(ins):
        heads = jnp.swapaxes(x[...], 0, 1)
        lead[:, a] = heads[:, :-quarter]
        rest[:, a] = heads[:, quarter:]


def pack_rest(arrays):
    rows, heads, hdim = arrays[0].shape
    shape = (heads, len(arrays), rows - rows // QUARTERS, hdim)
    return pl.pallas_call(
        pack_rest_kernel,
        out_shape=[jax.ShapeDtypeStruct(shape, jnp.bfloat16)] * 2,
        compiler_params=pltpu.CompilerParams(vmem_limit_bytes=60 * MIB),
        cost_estimate=pl.CostEstimate(flops=0, bytes_accessed=9 * MIB, transcendentals=0),
        name="pack_rest",
    )(*arrays)


def from_end(stage, stages):
    return jnp.minimum(stage, stages - 1 - stage)


def merge_kernel(size, stage, *refs):
    received, rest, out = refs[:-2], refs[-2], refs[-1]
    f = 0
    for x in received:
        for n in range(x.shape[2] // size):
            to, at = slice(f * size, (f + 1) * size), slice(n * size, (n + 1) * size)

            @pl.when(f < stage[1])
            def _():
                out[:, :, to] = x[:, :, at]

            @pl.when(f >= stage[1])
            def _():
                out[:, :, to] = rest[:, :, to]

            f += 1


def merge(stage, size, received, rest):
    in_vmem = pl.BlockSpec(memory_space=pltpu.VMEM)
    return pl.pallas_call(
        lambda *refs: merge_kernel(size, *refs),
        in_specs=[pl.BlockSpec(memory_space=pltpu.SMEM)] + [in_vmem] * (len(received) + 1),
        out_shape=jax.ShapeDtypeStruct(rest.shape, rest.dtype),
        compiler_params=pltpu.CompilerParams(vmem_limit_bytes=40 * MIB),
        cost_estimate=pl.CostEstimate(flops=0, bytes_accessed=8 * MIB, transcendentals=0),
        name="merge",
    )(stage, *received, rest)


def unpack_split_kernel(stage, own, late, out, x, heads, sem, out_sem):
    size = x.shape[2] // EIGHTHS
    halves = out_sem.shape[0]
    rows = x.shape[2] // halves

    def copy(ref, slot, e):
        return pltpu.make_async_copy(
            ref.at[:, :, pl.ds(slot * size, size)],
            x.at[:, :, pl.ds(e * size, size)],
            sem.at[e],
        )

    for e in range(EIGHTHS):
        if e < EIGHTHS - 1:
            pl.when(e < stage[1])(copy(own, e, e).start)
        pl.when(e >= stage[1])(copy(late, max(e - 1, 0), e).start)
    writes = []
    for h in range(halves):
        for e in range(h * EIGHTHS // halves, (h + 1) * EIGHTHS // halves):
            copy(own, 0, e).wait()
        at = pl.ds(h * rows, rows)
        for a in range(x.shape[1]):
            heads[a, h * rows : (h + 1) * rows] = jnp.swapaxes(
                x[:, a, h * rows : (h + 1) * rows], 0, 1
            )
        writes.append(pltpu.make_async_copy(heads.at[:, at], out.at[:, at], out_sem.at[h]))
        writes[-1].start()
    for write in writes:
        write.wait()


def unpack_split(stage, own, late):
    heads, count, some, hdim = own.shape
    rows = some * EIGHTHS // (EIGHTHS - 1)
    anywhere = pl.BlockSpec(memory_space=pl.ANY)
    return pl.pallas_call(
        unpack_split_kernel,
        in_specs=[pl.BlockSpec(memory_space=pltpu.SMEM), anywhere, anywhere],
        out_specs=anywhere,
        out_shape=jax.ShapeDtypeStruct((count, rows, heads, hdim), jnp.bfloat16),
        scratch_shapes=[
            pltpu.VMEM((heads, count, rows, hdim), jnp.bfloat16),
            pltpu.VMEM((count, rows, heads, hdim), jnp.bfloat16),
            pltpu.SemaphoreType.DMA((EIGHTHS,)),
            pltpu.SemaphoreType.DMA((2,)),
        ],
        compiler_params=pltpu.CompilerParams(vmem_limit_bytes=40 * MIB),
        cost_estimate=pl.CostEstimate(flops=0, bytes_accessed=6 * MIB, transcendentals=0),
        name="unpack_split",
    )(stage, own, late)


def outward(stages):
    half = stages // 2
    return [(p, p - 1) for p in range(1, half)] + [(p, p + 1) for p in range(half, stages - 1)]


def unpack_kernel(x, out):
    for a in range(x.shape[1]):
        out[a] = jnp.swapaxes(x[:, a], 0, 1)


def unpack(x):
    heads, count, rows, hdim = x.shape
    chunk = rows // 2
    return pl.pallas_call(
        unpack_kernel,
        grid=(rows // chunk,),
        in_specs=[pl.BlockSpec((heads, count, chunk, hdim), lambda i: (0, 0, i, 0))],
        out_specs=pl.BlockSpec((count, chunk, heads, hdim), lambda i: (0, i, 0, 0)),
        out_shape=jax.ShapeDtypeStruct((count, rows, heads, hdim), jnp.bfloat16),
        compiler_params=pltpu.CompilerParams(vmem_limit_bytes=60 * MIB),
        cost_estimate=pl.CostEstimate(
            flops=0, bytes_accessed=4 * count * rows * heads * hdim, transcendentals=0
        ),
        name="unpack",
    )(x)


def tie_kernel(x, first, out):
    del x, first, out


def after(x, first):
    anywhere = pl.BlockSpec(memory_space=pl.ANY)
    return pl.pallas_call(
        tie_kernel,
        in_specs=[anywhere, anywhere],
        out_specs=anywhere,
        out_shape=jax.ShapeDtypeStruct(x.shape, x.dtype),
        input_output_aliases={0: 0},
        name="after",
    )(x, first)


def dot(a, b, dims):
    return lax.dot_general(a, b, (dims, ((), ())), preferred_element_type=jnp.float32)


def block(ref, a, b):
    per = ref.shape[2] // BLK
    return ref[b // per, a, pl.ds(pl.multiple_of((b % per) * BLK, BLK), BLK), :]


def gather(x, a, picks):
    return jnp.concatenate([block(x, a, b) for b in picks], axis=0)


def probabilities(scores, bias):
    scores = [s * (SCALE * LOG2E) + b for s, b in zip(scores, bias)]
    weights = [jnp.exp2(s - jnp.max(s, axis=-1, keepdims=True)) for s in scores]
    return [w * (1.0 / jnp.sum(w, axis=-1, keepdims=True)) for w in weights]


def step_blocks(t, ids, x):
    per = x.shape[2] // BLK
    blocks = [t * STEP + n for n in range(STEP)]
    picks = [[ids[i, c] for c in range(SLOTS)] for i in blocks]
    places = [
        (t * (STEP // per) + n // per, slice((n % per) * BLK, (n % per + 1) * BLK))
        for n in range(STEP)
    ]
    return blocks, picks, places


def forward_kernel(stages, stage, ids, bias, whole, own, back, first, out, x):
    del first
    edge = from_end(stage[0], stages)
    lent = QUARTERS - edge
    quarter = x.shape[2] // QUARTERS

    @pl.when(edge == 0)
    def _():
        x[...] = whole[:, :3]

    for e in range(QUARTERS):
        to = slice(e * quarter, (e + 1) * quarter)

        if e < QUARTERS - 1:

            @pl.when((edge > 0) & (e < lent))
            def _():
                x[:, :, to] = back[:, :, to]

        if e > 0:

            @pl.when((edge > 0) & (e >= lent))
            def _():
                x[:, :, to] = own[:, :, (e - 1) * quarter : e * quarter]

    def step(t, carry):
        blocks, picks, places = step_blocks(t, ids, x)
        keys = [gather(x, 1, p) for p in picks]
        values = [gather(x, 2, p) for p in picks]
        queries = [x[j, 0, own, :] for j, own in places]
        scores = [dot(q, k, ((1,), (1,))) for q, k in zip(queries, keys)]
        prob = probabilities(scores, [bias[pl.ds(i, 1), :] for i in blocks])
        prob = [p.astype(jnp.bfloat16) for p in prob]
        for (j, own), p, v in zip(places, prob, values):
            out[j, 0, own, :] = dot(p, v, ((1,), (0,))).astype(jnp.bfloat16)
        return carry

    lax.fori_loop(0, ids.shape[0] // STEP, step, 0)


def backward_kernel(stages, stage, ids, bias, x, lead, last, rest, dk, dv):
    del stages, stage
    parts, _, rows, hdim = x.shape
    size = rows // EIGHTHS
    ranges = [(lead, 0), (last, rows - 2 * size), (rest, size)]

    def put(j, a, at, rows_of):
        count = rows_of.shape[-2]
        for out, start in ranges:
            low, high = max(at, start), min(at + count, start + out.shape[2])
            if low < high:
                out[j, a, low - start : high - start, :] = rows_of[..., low - at : high - at, :]

    dk[...] = jnp.zeros_like(dk)
    dv[...] = jnp.zeros_like(dv)

    def step(t, carry):
        blocks, picks, places = step_blocks(t, ids, x)
        keys = [gather(x, 1, p) for p in picks]
        values = [gather(x, 2, p) for p in picks]
        queries = [x[j, 0, own, :] for j, own in places]
        grads = [x[j, 3, own, :] for j, own in places]
        scores = [dot(q, k, ((1,), (1,))) for q, k in zip(queries, keys)]
        dprob = [dot(g, v, ((1,), (1,))) for g, v in zip(grads, values)]
        prob = probabilities(scores, [bias[pl.ds(i, 1), :] for i in blocks])
        prob_b = [p.astype(jnp.bfloat16) for p in prob]
        value_part = [dot(p, g, ((0,), (0,))) for p, g in zip(prob_b, grads)]
        delta = [
            jnp.sum(p.astype(jnp.float32) * d, axis=-1, keepdims=True)
            for p, d in zip(prob_b, dprob)
        ]
        dscore = [
            (p * ((d - e) * SCALE)).astype(jnp.bfloat16) for p, d, e in zip(prob, dprob, delta)
        ]
        key_part = [dot(d, q, ((0,), (0,))) for d, q in zip(dscore, queries)]
        for (j, own), d, k in zip(places, dscore, keys):
            put(j, 0, own.start, dot(d, k, ((1,), (0,))).astype(jnp.bfloat16))
        for pick, kp, vp in zip(picks, key_part, value_part):
            for c, b in enumerate(pick):
                at = pl.ds(pl.multiple_of(b * BLK, BLK), BLK)
                dk[at, :] += kp[c * BLK : (c + 1) * BLK]
                dv[at, :] += vp[c * BLK : (c + 1) * BLK]
        return carry

    lax.fori_loop(0, ids.shape[0] // STEP, step, 0)
    put(slice(None), 1, 0, dk[...].reshape(parts, rows, hdim).astype(jnp.bfloat16))
    put(slice(None), 2, 0, dv[...].reshape(parts, rows, hdim).astype(jnp.bfloat16))


def attention(kernel, results, lengths, stage, ids, bias, ins, rest, scratch, matmuls):
    parts, _, rows, hdim = ins[0].shape
    work = parts * rows * SLOTS * BLK * hdim * 2
    stages = lax.axis_size("pipe")
    in_smem = pl.BlockSpec(memory_space=pltpu.SMEM)
    in_vmem = pl.BlockSpec(memory_space=pltpu.VMEM)
    return pl.pallas_call(
        lambda *refs: kernel(stages, *refs),
        out_shape=[
            jax.ShapeDtypeStruct((parts, results, n, hdim), jnp.bfloat16) for n in lengths
        ],
        in_specs=[in_smem, in_smem, in_vmem]
        + [in_vmem] * len(ins)
        + [pl.BlockSpec(memory_space=pl.ANY)] * len(rest),
        scratch_shapes=scratch,
        compiler_params=pltpu.CompilerParams(vmem_limit_bytes=40 * MIB),
        cost_estimate=pl.CostEstimate(
            flops=4 * matmuls * work, bytes_accessed=8 * MIB, transcendentals=0
        ),
        name=kernel.__name__,
    )(stage, ids, bias, *ins, *rest)


def exchange(x):
    return lax.all_to_all(x, ("seq", "tp"), split_axis=0, concat_axis=0, tiled=True)


def slots_and_bias(glob, win, count, rand_ids):
    ids, opened = key_slots(glob, win, count, rand_ids)
    bias = jnp.where(jnp.repeat(opened, BLK, axis=1), 0.0, -1e30).astype(jnp.float32)
    return ids, bias


def body(
    query_fwd,
    key_fwd,
    value_fwd,
    query_bwd,
    key_bwd,
    value_bwd,
    grad_mix,
    global_blocks,
    window,
    rand_count,
    rand_blocks,
):
    ids, bias = slots_and_bias(
        global_blocks[0, 0], window[0, 0], rand_count[0, 0], rand_blocks[0, 0]
    )
    stages = lax.axis_size("pipe")
    stage = lax.axis_index("pipe").astype(jnp.int32)[None]
    front = (query_fwd[0], key_fwd[0], value_fwd[0])
    first = exchange(
        pack_first(stage, (query_bwd[0], key_bwd[0], value_bwd[0], grad_mix[0]), front)
    )
    lead, rest = pack_rest(front)
    received = lax.ppermute(lead, "pipe", outward(stages))
    parts, _, rows, _ = first.shape
    quarter, eighth = rows // QUARTERS, rows // EIGHTHS
    lent = jnp.concatenate([stage, QUARTERS - 1 - from_end(stage, stages)])
    second = merge(lent, quarter, [received], rest)
    second, ids, bias = lax.optimization_barrier((second, ids, bias))
    second = exchange(second)
    early, last, rest = attention(
        backward_kernel, 3, [rows - 2 * eighth, eighth, rows - eighth],
        stage, ids, bias, [first], [], [pltpu.VMEM((parts * rows, HDIM), jnp.float32)] * 2, 5,
    )
    early = passed_along(early, "pipe", -1)
    last = lax.ppermute(last, "pipe", [(1, 0)])
    lent = jnp.concatenate([stage, EIGHTHS - 1 - stage])
    grads = merge(lent, eighth, [early, last], rest)
    back = lax.ppermute(second, "pipe", [(b, a) for a, b in outward(stages)])
    (mixed,) = attention(
        forward_kernel, 1, [rows], stage, ids, bias, [first, second, back], [grads],
        [pltpu.VMEM((parts, 3, rows, HDIM), jnp.bfloat16)], 2,
    )
    mixed = passed_along(mixed, "pipe", 1)
    grads = exchange(grads)
    late = passed_along(grads, "pipe", -1)
    mixed = exchange(after(mixed, grads))
    return (unpack(mixed), unpack_split(lent, grads, late)[:, None])


def solution(mesh):
    rows = P("pipe", ("seq", "tp"), None, None)
    placed = (rows,) * 7 + (
        P("pipe", ("seq", "tp"), None),
        P("pipe", ("seq", "tp")),
        P("pipe", ("seq", "tp")),
        P("pipe", ("seq", "tp"), None, None),
    )
    return jax.shard_map(
        body,
        mesh=mesh,
        in_specs=placed,
        out_specs=(rows, P(None, "pipe", ("seq", "tp"), None, None)),
        check_vma=False,
    )
```

```python
import math

import jax
import jax.numpy as jnp
from jax import lax
from jax.experimental import pallas as pl
from jax.experimental.pallas import tpu as pltpu
from jax.sharding import PartitionSpec as P

BLK = 64
GLOBAL = 2
WMAX = 1
R_MOST = 3
SLOTS = 8
HDIM = 128
SCALE = HDIM ** (-0.5)
LOG2E = math.log2(math.e)
MIB = 1 << 20
STEP = 8
QUARTERS = 4
EIGHTHS = 8


def passed_along(value, axis, steps):
    count = lax.axis_size(axis)
    first, last = (max(0, -steps), min(count, count - steps))
    return lax.ppermute(value, axis, [(source, source + steps) for source in range(first, last)])


def key_slots(glob, win, count, rand_ids):
    nblk = rand_ids.shape[0]
    blocks = jnp.arange(nblk, dtype=jnp.int32)[:, None]
    glob_ids = jnp.broadcast_to(glob[None, :], (nblk, GLOBAL))
    glob_open = jnp.ones((nblk, GLOBAL), jnp.bool_)
    offsets = jnp.arange(-WMAX, WMAX + 1, dtype=jnp.int32)[None, :]
    near = blocks + offsets
    near_open = (jnp.abs(offsets) <= win) & (near >= 0) & (near < nblk)
    near = jnp.clip(near, 0, nblk - 1)
    rand_open = jnp.broadcast_to(
        jnp.arange(R_MOST, dtype=jnp.int32)[None, :] < count, (nblk, R_MOST)
    )
    ids = jnp.concatenate([glob_ids, near, rand_ids], axis=1)
    opened = jnp.concatenate([glob_open, near_open, rand_open], axis=1)
    same = ids[:, :, None] == ids[:, None, :]
    earlier = jnp.arange(SLOTS)[None, :] < jnp.arange(SLOTS)[:, None]
    repeated = jnp.any(same & opened[:, None, :] & earlier[None], axis=2)
    return (ids, opened & jnp.logical_not(repeated))


def pack_first_kernel(stage, *refs):
    back, front, out, (wide, heads, sem, out_sem) = refs[:4], refs[4:7], refs[7], refs[8:]
    rows = back[0].shape[0]
    chunks = sem.shape[1]
    size = rows // chunks

    def copy(x, a, c):
        at = pl.ds(c * size, size)
        return pltpu.make_async_copy(x.at[at], wide.at[a, at], sem.at[a, c])

    @pl.when(stage[0] != 0)
    def _():
        for c in range(chunks):
            for a in range(4):
                copy(back[a], a, c).start()

    @pl.when(stage[0] == 0)
    def _():
        for c in range(chunks):
            for a in range(4):
                copy(front[min(a, 2)], a, c).start()

    writes = []
    for c in range(chunks):
        at = pl.ds(c * size, size)
        for a in range(4):
            copy(back[a], a, c).wait()
            heads[:, a, c * size : (c + 1) * size] = jnp.swapaxes(
                wide[a, c * size : (c + 1) * size], 0, 1
            )
        writes.append(pltpu.make_async_copy(heads.at[:, :, at], out.at[:, :, at], out_sem.at[c]))
        writes[-1].start()
    for write in writes:
        write.wait()


def pack_first(stage, back, front):
    rows, heads, hdim = back[0].shape
    return pl.pallas_call(
        pack_first_kernel,
        in_specs=[pl.BlockSpec(memory_space=pltpu.SMEM)]
        + [pl.BlockSpec(memory_space=pl.ANY)] * 7,
        out_specs=pl.BlockSpec(memory_space=pl.ANY),
        out_shape=jax.ShapeDtypeStruct((heads, 4, rows, hdim), jnp.bfloat16),
        scratch_shapes=[
            pltpu.VMEM((4, rows, heads, hdim), jnp.bfloat16),
            pltpu.VMEM((heads, 4, rows, hdim), jnp.bfloat16),
            pltpu.SemaphoreType.DMA((4, 4)),
            pltpu.SemaphoreType.DMA((4,)),
        ],
        compiler_params=pltpu.CompilerParams(vmem_limit_bytes=60 * MIB),
        name="pack_first",
    )(stage, *back, *front)


def pack_rest_kernel(*refs):
    ins, lead, rest = refs[:-2], refs[-2], refs[-1]
    quarter = ins[0].shape[0] // QUARTERS
    for a, x in enumerate(ins):
        heads = jnp.swapaxes(x[...], 0, 1)
        lead[:, a] = heads[:, :-quarter]
        rest[:, a] = heads[:, quarter:]


def pack_rest(arrays):
    rows, heads, hdim = arrays[0].shape
    shape = (heads, len(arrays), rows - rows // QUARTERS, hdim)
    return pl.pallas_call(
        pack_rest_kernel,
        out_shape=[jax.ShapeDtypeStruct(shape, jnp.bfloat16)] * 2,
        compiler_params=pltpu.CompilerParams(vmem_limit_bytes=60 * MIB),
        cost_estimate=pl.CostEstimate(flops=0, bytes_accessed=9 * MIB, transcendentals=0),
        name="pack_rest",
    )(*arrays)


def from_end(stage, stages):
    return jnp.minimum(stage, stages - 1 - stage)


def merge_kernel(size, stage, *refs):
    received, rest, out = refs[:-2], refs[-2], refs[-1]
    f = 0
    for x in received:
        for n in range(x.shape[2] // size):
            to, at = slice(f * size, (f + 1) * size), slice(n * size, (n + 1) * size)

            @pl.when(f < stage[1])
            def _():
                out[:, :, to] = x[:, :, at]

            @pl.when(f >= stage[1])
            def _():
                out[:, :, to] = rest[:, :, to]

            f += 1


def merge(stage, size, received, rest):
    in_vmem = pl.BlockSpec(memory_space=pltpu.VMEM)
    return pl.pallas_call(
        lambda *refs: merge_kernel(size, *refs),
        in_specs=[pl.BlockSpec(memory_space=pltpu.SMEM)] + [in_vmem] * (len(received) + 1),
        out_shape=jax.ShapeDtypeStruct(rest.shape, rest.dtype),
        compiler_params=pltpu.CompilerParams(vmem_limit_bytes=40 * MIB),
        cost_estimate=pl.CostEstimate(flops=0, bytes_accessed=8 * MIB, transcendentals=0),
        name="merge",
    )(stage, *received, rest)


def unpack_kernel(stage, own, late, mixed, out, mixed_out, x, heads, mixed_heads, sem, out_sem):
    steps = out_sem.shape[0] - 1
    size = x.shape[2] // (EIGHTHS - 1)
    rows = heads.shape[1] // steps

    def copy(e):
        at = pl.ds(e * size, size)
        return pltpu.make_async_copy(own.at[:, :, at], x.at[:, :, at], sem.at[e])

    def put(ref, slot, e):
        for a in range(heads.shape[0]):
            heads[a, e * size : (e + 1) * size] = jnp.swapaxes(
                ref[:, a, slot * size : (slot + 1) * size], 0, 1
            )

    for e in range(EIGHTHS - 1):
        pl.when(e < stage[1])(copy(e).start)
    mixed_heads[...] = jnp.swapaxes(mixed[:, 0], 0, 1)
    writes = [pltpu.make_async_copy(mixed_heads, mixed_out.at[0], out_sem.at[steps])]
    writes[-1].start()
    for h in range(steps):
        for e in range(h * EIGHTHS // steps, (h + 1) * EIGHTHS // steps):
            if e < EIGHTHS - 1:

                @pl.when(e < stage[1])
                def _():
                    copy(e).wait()
                    put(x, e, e)

            @pl.when(e >= stage[1])
            def _():
                put(late, max(e - 1, 0), e)

        at = pl.ds(h * rows, rows)
        writes.append(pltpu.make_async_copy(heads.at[:, at], out.at[:, at], out_sem.at[h]))
        writes[-1].start()
    for write in writes:
        write.wait()


def unpack(stage, own, late, mixed):
    heads, count, some, hdim = own.shape
    rows = some * EIGHTHS // (EIGHTHS - 1)
    anywhere = pl.BlockSpec(memory_space=pl.ANY)
    in_vmem = pl.BlockSpec(memory_space=pltpu.VMEM)
    return pl.pallas_call(
        unpack_kernel,
        in_specs=[pl.BlockSpec(memory_space=pltpu.SMEM), anywhere, in_vmem, in_vmem],
        out_specs=[anywhere] * 2,
        out_shape=[
            jax.ShapeDtypeStruct((count, rows, heads, hdim), jnp.bfloat16),
            jax.ShapeDtypeStruct((1, rows, heads, hdim), jnp.bfloat16),
        ],
        scratch_shapes=[
            pltpu.VMEM((heads, count, some, hdim), jnp.bfloat16),
            pltpu.VMEM((count, rows, heads, hdim), jnp.bfloat16),
            pltpu.VMEM((rows, heads, hdim), jnp.bfloat16),
            pltpu.SemaphoreType.DMA((EIGHTHS - 1,)),
            pltpu.SemaphoreType.DMA((4 + 1,)),
        ],
        compiler_params=pltpu.CompilerParams(vmem_limit_bytes=32 * MIB),
        cost_estimate=pl.CostEstimate(flops=0, bytes_accessed=8 * MIB, transcendentals=0),
        name="unpack",
    )(stage, own, late, mixed)


def outward(stages):
    half = stages // 2
    return [(p, p - 1) for p in range(1, half)] + [(p, p + 1) for p in range(half, stages - 1)]


def dot(a, b, dims):
    return lax.dot_general(a, b, (dims, ((), ())), preferred_element_type=jnp.float32)


def block(ref, a, b):
    per = ref.shape[2] // BLK
    return ref[b // per, a, pl.ds(pl.multiple_of((b % per) * BLK, BLK), BLK), :]


def gather(x, a, picks):
    return jnp.concatenate([block(x, a, b) for b in picks], axis=0)


def probabilities(scores, bias):
    scores = [s * (SCALE * LOG2E) + b for s, b in zip(scores, bias)]
    weights = [jnp.exp2(s - jnp.max(s, axis=-1, keepdims=True)) for s in scores]
    return [w * (1.0 / jnp.sum(w, axis=-1, keepdims=True)) for w in weights]


def step_blocks(t, ids, x):
    per = x.shape[2] // BLK
    blocks = [t * STEP + n for n in range(STEP)]
    picks = [[ids[i, c] for c in range(SLOTS)] for i in blocks]
    places = [
        (t * (STEP // per) + n // per, slice((n % per) * BLK, (n % per + 1) * BLK))
        for n in range(STEP)
    ]
    return blocks, picks, places


def forward_kernel(stages, stage, ids, bias, whole, own, back, first, out, x):
    del first
    edge = from_end(stage[0], stages)
    lent = QUARTERS - edge
    quarter = x.shape[2] // QUARTERS

    @pl.when(edge == 0)
    def _():
        x[...] = whole[:, :3]

    for e in range(QUARTERS):
        to = slice(e * quarter, (e + 1) * quarter)

        if e < QUARTERS - 1:

            @pl.when((edge > 0) & (e < lent))
            def _():
                x[:, :, to] = back[:, :, to]

        if e > 0:

            @pl.when((edge > 0) & (e >= lent))
            def _():
                x[:, :, to] = own[:, :, (e - 1) * quarter : e * quarter]

    def step(t, carry):
        blocks, picks, places = step_blocks(t, ids, x)
        keys = [gather(x, 1, p) for p in picks]
        values = [gather(x, 2, p) for p in picks]
        queries = [x[j, 0, own, :] for j, own in places]
        scores = [dot(q, k, ((1,), (1,))) for q, k in zip(queries, keys)]
        prob = probabilities(scores, [bias[pl.ds(i, 1), :] for i in blocks])
        prob = [p.astype(jnp.bfloat16) for p in prob]
        for (j, own), p, v in zip(places, prob, values):
            out[j, 0, own, :] = dot(p, v, ((1,), (0,))).astype(jnp.bfloat16)
        return carry

    lax.fori_loop(0, ids.shape[0] // STEP, step, 0)


def backward_kernel(stages, stage, ids, bias, x, lead, last, rest, dk, dv):
    del stages, stage
    parts, _, rows, hdim = x.shape
    size = rows // EIGHTHS
    ranges = [(lead, 0), (last, rows - 2 * size), (rest, size)]

    def put(j, a, at, rows_of):
        count = rows_of.shape[-2]
        for out, start in ranges:
            low, high = max(at, start), min(at + count, start + out.shape[2])
            if low < high:
                out[j, a, low - start : high - start, :] = rows_of[..., low - at : high - at, :]

    dk[...] = jnp.zeros_like(dk)
    dv[...] = jnp.zeros_like(dv)

    def step(t, carry):
        blocks, picks, places = step_blocks(t, ids, x)
        keys = [gather(x, 1, p) for p in picks]
        values = [gather(x, 2, p) for p in picks]
        queries = [x[j, 0, own, :] for j, own in places]
        grads = [x[j, 3, own, :] for j, own in places]
        scores = [dot(q, k, ((1,), (1,))) for q, k in zip(queries, keys)]
        dprob = [dot(g, v, ((1,), (1,))) for g, v in zip(grads, values)]
        prob = probabilities(scores, [bias[pl.ds(i, 1), :] for i in blocks])
        prob_b = [p.astype(jnp.bfloat16) for p in prob]
        value_part = [dot(p, g, ((0,), (0,))) for p, g in zip(prob_b, grads)]
        delta = [
            jnp.sum(p.astype(jnp.float32) * d, axis=-1, keepdims=True)
            for p, d in zip(prob_b, dprob)
        ]
        dscore = [
            (p * ((d - e) * SCALE)).astype(jnp.bfloat16) for p, d, e in zip(prob, dprob, delta)
        ]
        key_part = [dot(d, q, ((0,), (0,))) for d, q in zip(dscore, queries)]
        for (j, own), d, k in zip(places, dscore, keys):
            put(j, 0, own.start, dot(d, k, ((1,), (0,))).astype(jnp.bfloat16))
        for pick, kp, vp in zip(picks, key_part, value_part):
            for c, b in enumerate(pick):
                at = pl.ds(pl.multiple_of(b * BLK, BLK), BLK)
                dk[at, :] += kp[c * BLK : (c + 1) * BLK]
                dv[at, :] += vp[c * BLK : (c + 1) * BLK]
        return carry

    lax.fori_loop(0, ids.shape[0] // STEP, step, 0)
    put(slice(None), 1, 0, dk[...].reshape(parts, rows, hdim).astype(jnp.bfloat16))
    put(slice(None), 2, 0, dv[...].reshape(parts, rows, hdim).astype(jnp.bfloat16))


def attention(kernel, results, lengths, stage, ids, bias, ins, rest, scratch, matmuls):
    parts, _, rows, hdim = ins[0].shape
    work = parts * rows * SLOTS * BLK * hdim * 2
    stages = lax.axis_size("pipe")
    in_smem = pl.BlockSpec(memory_space=pltpu.SMEM)
    in_vmem = pl.BlockSpec(memory_space=pltpu.VMEM)
    return pl.pallas_call(
        lambda *refs: kernel(stages, *refs),
        out_shape=[
            jax.ShapeDtypeStruct((parts, results, n, hdim), jnp.bfloat16) for n in lengths
        ],
        in_specs=[in_smem, in_smem, in_vmem]
        + [in_vmem] * len(ins)
        + [pl.BlockSpec(memory_space=pl.ANY)] * len(rest),
        scratch_shapes=scratch,
        compiler_params=pltpu.CompilerParams(vmem_limit_bytes=40 * MIB),
        cost_estimate=pl.CostEstimate(
            flops=4 * matmuls * work, bytes_accessed=8 * MIB, transcendentals=0
        ),
        name=kernel.__name__,
    )(stage, ids, bias, *ins, *rest)


def exchange(x):
    return lax.all_to_all(x, ("seq", "tp"), split_axis=0, concat_axis=0, tiled=True)


def slots_and_bias(glob, win, count, rand_ids):
    ids, opened = key_slots(glob, win, count, rand_ids)
    bias = jnp.where(jnp.repeat(opened, BLK, axis=1), 0.0, -1e30).astype(jnp.float32)
    return ids, bias


def body(
    query_fwd,
    key_fwd,
    value_fwd,
    query_bwd,
    key_bwd,
    value_bwd,
    grad_mix,
    global_blocks,
    window,
    rand_count,
    rand_blocks,
):
    ids, bias = slots_and_bias(
        global_blocks[0, 0], window[0, 0], rand_count[0, 0], rand_blocks[0, 0]
    )
    stages = lax.axis_size("pipe")
    stage = lax.axis_index("pipe").astype(jnp.int32)[None]
    front = (query_fwd[0], key_fwd[0], value_fwd[0])
    first = exchange(
        pack_first(stage, (query_bwd[0], key_bwd[0], value_bwd[0], grad_mix[0]), front)
    )
    lead, rest = pack_rest(front)
    received = lax.ppermute(lead, "pipe", outward(stages))
    parts, _, rows, _ = first.shape
    quarter, eighth = rows // QUARTERS, rows // EIGHTHS
    lent = jnp.concatenate([stage, QUARTERS - 1 - from_end(stage, stages)])
    second = merge(lent, quarter, [received], rest)
    second, ids, bias = lax.optimization_barrier((second, ids, bias))
    second = exchange(second)
    early, last, rest = attention(
        backward_kernel, 3, [rows - 2 * eighth, eighth, rows - eighth],
        stage, ids, bias, [first], [], [pltpu.VMEM((parts * rows, HDIM), jnp.float32)] * 2, 5,
    )
    early = passed_along(early, "pipe", -1)
    last = lax.ppermute(last, "pipe", [(1, 0)])
    lent = jnp.concatenate([stage, EIGHTHS - 1 - stage])
    grads = merge(lent, eighth, [early, last], rest)
    back = lax.ppermute(second, "pipe", [(b, a) for a, b in outward(stages)])
    (mixed,) = attention(
        forward_kernel, 1, [rows], stage, ids, bias, [first, second, back], [grads],
        [pltpu.VMEM((parts, 3, rows, HDIM), jnp.bfloat16)], 2,
    )
    mixed = passed_along(mixed, "pipe", 1)
    grads = exchange(grads)
    late = passed_along(grads, "pipe", -1)
    mixed = exchange(mixed)
    grads, mixed = unpack(lent, grads, late, mixed)
    return (mixed, grads[:, None])


def solution(mesh):
    rows = P("pipe", ("seq", "tp"), None, None)
    placed = (rows,) * 7 + (
        P("pipe", ("seq", "tp"), None),
        P("pipe", ("seq", "tp")),
        P("pipe", ("seq", "tp")),
        P("pipe", ("seq", "tp"), None, None),
    )
    return jax.shard_map(
        body,
        mesh=mesh,
        in_specs=placed,
        out_specs=(rows, P(None, "pipe", ("seq", "tp"), None, None)),
        check_vma=False,
    )
```

```python
import math

import jax
import jax.numpy as jnp
from jax import lax
from jax.experimental import pallas as pl
from jax.experimental.pallas import tpu as pltpu
from jax.sharding import PartitionSpec as P

BLK = 64
GLOBAL = 2
WMAX = 1
R_MOST = 3
SLOTS = 8
HDIM = 128
SCALE = HDIM ** (-0.5)
LOG2E = math.log2(math.e)
MIB = 1 << 20
STEP = 8
QUARTERS = 4
EIGHTHS = 8


def passed_along(value, axis, steps):
    count = lax.axis_size(axis)
    first, last = (max(0, -steps), min(count, count - steps))
    return lax.ppermute(value, axis, [(source, source + steps) for source in range(first, last)])


def key_slots(glob, win, count, rand_ids):
    nblk = rand_ids.shape[0]
    blocks = jnp.arange(nblk, dtype=jnp.int32)[:, None]
    glob_ids = jnp.broadcast_to(glob[None, :], (nblk, GLOBAL))
    glob_open = jnp.ones((nblk, GLOBAL), jnp.bool_)
    offsets = jnp.arange(-WMAX, WMAX + 1, dtype=jnp.int32)[None, :]
    near = blocks + offsets
    near_open = (jnp.abs(offsets) <= win) & (near >= 0) & (near < nblk)
    near = jnp.clip(near, 0, nblk - 1)
    rand_open = jnp.broadcast_to(
        jnp.arange(R_MOST, dtype=jnp.int32)[None, :] < count, (nblk, R_MOST)
    )
    ids = jnp.concatenate([glob_ids, near, rand_ids], axis=1)
    opened = jnp.concatenate([glob_open, near_open, rand_open], axis=1)
    same = ids[:, :, None] == ids[:, None, :]
    earlier = jnp.arange(SLOTS)[None, :] < jnp.arange(SLOTS)[:, None]
    repeated = jnp.any(same & opened[:, None, :] & earlier[None], axis=2)
    return (ids, opened & jnp.logical_not(repeated))


def pack_first_kernel(stage, *refs):
    back, front, out, (wide, heads, sem, out_sem) = refs[:4], refs[4:7], refs[7], refs[8:]
    rows = back[0].shape[0]
    chunks = sem.shape[1]
    size = rows // chunks

    def copy(x, a, c):
        at = pl.ds(c * size, size)
        return pltpu.make_async_copy(x.at[at], wide.at[a, at], sem.at[a, c])

    @pl.when(stage[0] != 0)
    def _():
        for c in range(chunks):
            for a in range(4):
                copy(back[a], a, c).start()

    @pl.when(stage[0] == 0)
    def _():
        for c in range(chunks):
            for a in range(4):
                copy(front[min(a, 2)], a, c).start()

    writes = []
    for c in range(chunks):
        at = pl.ds(c * size, size)
        for a in range(4):
            copy(back[a], a, c).wait()
            heads[:, a, c * size : (c + 1) * size] = jnp.swapaxes(
                wide[a, c * size : (c + 1) * size], 0, 1
            )
        writes.append(pltpu.make_async_copy(heads.at[:, :, at], out.at[:, :, at], out_sem.at[c]))
        writes[-1].start()
    for write in writes:
        write.wait()


def pack_first(stage, back, front):
    rows, heads, hdim = back[0].shape
    return pl.pallas_call(
        pack_first_kernel,
        in_specs=[pl.BlockSpec(memory_space=pltpu.SMEM)]
        + [pl.BlockSpec(memory_space=pl.ANY)] * 7,
        out_specs=pl.BlockSpec(memory_space=pl.ANY),
        out_shape=jax.ShapeDtypeStruct((heads, 4, rows, hdim), jnp.bfloat16),
        scratch_shapes=[
            pltpu.VMEM((4, rows, heads, hdim), jnp.bfloat16),
            pltpu.VMEM((heads, 4, rows, hdim), jnp.bfloat16),
            pltpu.SemaphoreType.DMA((4, 4)),
            pltpu.SemaphoreType.DMA((4,)),
        ],
        compiler_params=pltpu.CompilerParams(vmem_limit_bytes=60 * MIB),
        name="pack_first",
    )(stage, *back, *front)


def pack_rest_kernel(*refs):
    ins, lead, rest = refs[:-2], refs[-2], refs[-1]
    quarter = ins[0].shape[0] // QUARTERS
    for a, x in enumerate(ins):
        heads = jnp.swapaxes(x[...], 0, 1)
        lead[:, a] = heads[:, :-quarter]
        rest[:, a] = heads[:, quarter:]


def pack_rest(arrays):
    rows, heads, hdim = arrays[0].shape
    shape = (heads, len(arrays), rows - rows // QUARTERS, hdim)
    return pl.pallas_call(
        pack_rest_kernel,
        out_shape=[jax.ShapeDtypeStruct(shape, jnp.bfloat16)] * 2,
        compiler_params=pltpu.CompilerParams(vmem_limit_bytes=60 * MIB),
        cost_estimate=pl.CostEstimate(flops=0, bytes_accessed=9 * MIB, transcendentals=0),
        name="pack_rest",
    )(*arrays)


def from_end(stage, stages):
    return jnp.minimum(stage, stages - 1 - stage)


def merge_kernel(size, stage, *refs):
    received, rest, out = refs[:-2], refs[-2], refs[-1]
    f = 0
    for x in received:
        for n in range(x.shape[2] // size):
            to, at = slice(f * size, (f + 1) * size), slice(n * size, (n + 1) * size)

            @pl.when(f < stage[1])
            def _():
                out[:, :, to] = x[:, :, at]

            @pl.when(f >= stage[1])
            def _():
                out[:, :, to] = rest[:, :, to]

            f += 1


def merge(stage, size, received, rest):
    in_vmem = pl.BlockSpec(memory_space=pltpu.VMEM)
    return pl.pallas_call(
        lambda *refs: merge_kernel(size, *refs),
        in_specs=[pl.BlockSpec(memory_space=pltpu.SMEM)] + [in_vmem] * (len(received) + 1),
        out_shape=jax.ShapeDtypeStruct(rest.shape, rest.dtype),
        compiler_params=pltpu.CompilerParams(vmem_limit_bytes=40 * MIB),
        cost_estimate=pl.CostEstimate(flops=0, bytes_accessed=8 * MIB, transcendentals=0),
        name="merge",
    )(stage, *received, rest)


def unpack_kernel(stage, own, late, mixed, out, mixed_out, x, heads, mixed_heads, sem, out_sem):
    steps = out_sem.shape[0] - 1
    size = x.shape[2] // (EIGHTHS - 1)
    rows = heads.shape[1] // steps

    def copy(e):
        at = pl.ds(e * size, size)
        return pltpu.make_async_copy(own.at[:, :, at], x.at[:, :, at], sem.at[e])

    def put(ref, slot, e):
        for a in range(heads.shape[0]):
            heads[a, e * size : (e + 1) * size] = jnp.swapaxes(
                ref[:, a, slot * size : (slot + 1) * size], 0, 1
            )

    for e in range(EIGHTHS - 1):
        pl.when(e < stage[1])(copy(e).start)
    mixed_heads[...] = jnp.swapaxes(mixed[:, 0], 0, 1)
    writes = [pltpu.make_async_copy(mixed_heads, mixed_out.at[0], out_sem.at[steps])]
    writes[-1].start()
    for h in range(steps):
        for e in range(h * EIGHTHS // steps, (h + 1) * EIGHTHS // steps):
            if e < EIGHTHS - 1:

                @pl.when(e < stage[1])
                def _():
                    copy(e).wait()
                    put(x, e, e)

            @pl.when(e >= stage[1])
            def _():
                put(late, max(e - 1, 0), e)

        at = pl.ds(h * rows, rows)
        writes.append(pltpu.make_async_copy(heads.at[:, at], out.at[:, at], out_sem.at[h]))
        writes[-1].start()
    for write in writes:
        write.wait()


def unpack(stage, own, late, mixed):
    heads, count, some, hdim = own.shape
    rows = some * EIGHTHS // (EIGHTHS - 1)
    anywhere = pl.BlockSpec(memory_space=pl.ANY)
    in_vmem = pl.BlockSpec(memory_space=pltpu.VMEM)
    return pl.pallas_call(
        unpack_kernel,
        in_specs=[pl.BlockSpec(memory_space=pltpu.SMEM), anywhere, in_vmem, in_vmem],
        out_specs=[anywhere] * 2,
        out_shape=[
            jax.ShapeDtypeStruct((count, rows, heads, hdim), jnp.bfloat16),
            jax.ShapeDtypeStruct((1, rows, heads, hdim), jnp.bfloat16),
        ],
        scratch_shapes=[
            pltpu.VMEM((heads, count, some, hdim), jnp.bfloat16),
            pltpu.VMEM((count, rows, heads, hdim), jnp.bfloat16),
            pltpu.VMEM((rows, heads, hdim), jnp.bfloat16),
            pltpu.SemaphoreType.DMA((EIGHTHS - 1,)),
            pltpu.SemaphoreType.DMA((4 + 1,)),
        ],
        compiler_params=pltpu.CompilerParams(vmem_limit_bytes=32 * MIB),
        cost_estimate=pl.CostEstimate(flops=0, bytes_accessed=8 * MIB, transcendentals=0),
        name="unpack",
    )(stage, own, late, mixed)


def outward(stages):
    half = stages // 2
    return [(p, p - 1) for p in range(1, half)] + [(p, p + 1) for p in range(half, stages - 1)]


def dot(a, b, dims):
    return lax.dot_general(a, b, (dims, ((), ())), preferred_element_type=jnp.float32)


def block(ref, a, b):
    per = ref.shape[2] // BLK
    return ref[b // per, a, pl.ds(pl.multiple_of((b % per) * BLK, BLK), BLK), :]


def gather(x, a, picks):
    return jnp.concatenate([block(x, a, b) for b in picks], axis=0)


def probabilities(scores, bias):
    scores = [s * (SCALE * LOG2E) + b for s, b in zip(scores, bias)]
    weights = [jnp.exp2(s - jnp.max(s, axis=-1, keepdims=True)) for s in scores]
    return [w * (1.0 / jnp.sum(w, axis=-1, keepdims=True)) for w in weights]


def step_blocks(t, ids, x):
    per = x.shape[2] // BLK
    blocks = [t * STEP + n for n in range(STEP)]
    picks = [[ids[i, c] for c in range(SLOTS)] for i in blocks]
    places = [
        (t * (STEP // per) + n // per, slice((n % per) * BLK, (n % per + 1) * BLK))
        for n in range(STEP)
    ]
    return blocks, picks, places


def forward_kernel(stages, stage, ids, bias, whole, own, back, out, x, sem):
    edge = from_end(stage[0], stages)
    lent = QUARTERS - edge
    quarter = x.shape[2] // QUARTERS

    def copy(ref, f, e):
        return pltpu.make_async_copy(
            ref.at[:, pl.ds(0, x.shape[1]), pl.ds(f * quarter, quarter)],
            x.at[:, :, pl.ds(e * quarter, quarter)],
            sem.at[e],
        )

    for e in range(QUARTERS):
        pl.when(edge == 0)(copy(whole, e, e).start)
        if e < QUARTERS - 1:
            pl.when((edge > 0) & (e < lent))(copy(back, e, e).start)
        if e > 0:
            pl.when((edge > 0) & (e >= lent))(copy(own, e - 1, e).start)
    for e in range(QUARTERS):
        copy(whole, e, e).wait()

    def step(t, carry):
        blocks, picks, places = step_blocks(t, ids, x)
        keys = [gather(x, 1, p) for p in picks]
        values = [gather(x, 2, p) for p in picks]
        queries = [x[j, 0, own, :] for j, own in places]
        scores = [dot(q, k, ((1,), (1,))) for q, k in zip(queries, keys)]
        prob = probabilities(scores, [bias[pl.ds(i, 1), :] for i in blocks])
        prob = [p.astype(jnp.bfloat16) for p in prob]
        for (j, own), p, v in zip(places, prob, values):
            out[j, 0, own, :] = dot(p, v, ((1,), (0,))).astype(jnp.bfloat16)
        return carry

    lax.fori_loop(0, ids.shape[0] // STEP, step, 0)


def backward_kernel(stages, stage, ids, bias, x, lead, last, rest, dk, dv):
    del stages, stage
    parts, _, rows, hdim = x.shape
    size = rows // EIGHTHS
    ranges = [(lead, 0), (last, rows - 2 * size), (rest, size)]

    def put(j, a, at, rows_of):
        count = rows_of.shape[-2]
        for out, start in ranges:
            low, high = max(at, start), min(at + count, start + out.shape[2])
            if low < high:
                out[j, a, low - start : high - start, :] = rows_of[..., low - at : high - at, :]

    dk[...] = jnp.zeros_like(dk)
    dv[...] = jnp.zeros_like(dv)

    def step(t, carry):
        blocks, picks, places = step_blocks(t, ids, x)
        keys = [gather(x, 1, p) for p in picks]
        values = [gather(x, 2, p) for p in picks]
        queries = [x[j, 0, own, :] for j, own in places]
        grads = [x[j, 3, own, :] for j, own in places]
        scores = [dot(q, k, ((1,), (1,))) for q, k in zip(queries, keys)]
        dprob = [dot(g, v, ((1,), (1,))) for g, v in zip(grads, values)]
        prob = probabilities(scores, [bias[pl.ds(i, 1), :] for i in blocks])
        prob_b = [p.astype(jnp.bfloat16) for p in prob]
        value_part = [dot(p, g, ((0,), (0,))) for p, g in zip(prob_b, grads)]
        delta = [
            jnp.sum(p.astype(jnp.float32) * d, axis=-1, keepdims=True)
            for p, d in zip(prob_b, dprob)
        ]
        dscore = [
            (p * ((d - e) * SCALE)).astype(jnp.bfloat16) for p, d, e in zip(prob, dprob, delta)
        ]
        key_part = [dot(d, q, ((0,), (0,))) for d, q in zip(dscore, queries)]
        for (j, own), d, k in zip(places, dscore, keys):
            put(j, 0, own.start, dot(d, k, ((1,), (0,))).astype(jnp.bfloat16))
        for pick, kp, vp in zip(picks, key_part, value_part):
            for c, b in enumerate(pick):
                at = pl.ds(pl.multiple_of(b * BLK, BLK), BLK)
                dk[at, :] += kp[c * BLK : (c + 1) * BLK]
                dv[at, :] += vp[c * BLK : (c + 1) * BLK]
        return carry

    lax.fori_loop(0, ids.shape[0] // STEP, step, 0)
    put(slice(None), 1, 0, dk[...].reshape(parts, rows, hdim).astype(jnp.bfloat16))
    put(slice(None), 2, 0, dv[...].reshape(parts, rows, hdim).astype(jnp.bfloat16))


def attention(kernel, results, lengths, stage, ids, bias, ins, rest, scratch, matmuls):
    parts, _, rows, hdim = (*ins, *rest)[0].shape
    work = parts * rows * SLOTS * BLK * hdim * 2
    stages = lax.axis_size("pipe")
    in_smem = pl.BlockSpec(memory_space=pltpu.SMEM)
    in_vmem = pl.BlockSpec(memory_space=pltpu.VMEM)
    return pl.pallas_call(
        lambda *refs: kernel(stages, *refs),
        out_shape=[
            jax.ShapeDtypeStruct((parts, results, n, hdim), jnp.bfloat16) for n in lengths
        ],
        in_specs=[in_smem, in_smem, in_vmem]
        + [in_vmem] * len(ins)
        + [pl.BlockSpec(memory_space=pl.ANY)] * len(rest),
        scratch_shapes=scratch,
        compiler_params=pltpu.CompilerParams(vmem_limit_bytes=(40 if ins else 60) * MIB),
        cost_estimate=pl.CostEstimate(
            flops=4 * matmuls * work, bytes_accessed=8 * MIB, transcendentals=0
        ),
        name=kernel.__name__,
    )(stage, ids, bias, *ins, *rest)


def exchange(x):
    return lax.all_to_all(x, ("seq", "tp"), split_axis=0, concat_axis=0, tiled=True)


def slots_and_bias(glob, win, count, rand_ids):
    ids, opened = key_slots(glob, win, count, rand_ids)
    bias = jnp.where(jnp.repeat(opened, BLK, axis=1), 0.0, -1e30).astype(jnp.float32)
    return ids, bias


def body(
    query_fwd,
    key_fwd,
    value_fwd,
    query_bwd,
    key_bwd,
    value_bwd,
    grad_mix,
    global_blocks,
    window,
    rand_count,
    rand_blocks,
):
    ids, bias = slots_and_bias(
        global_blocks[0, 0], window[0, 0], rand_count[0, 0], rand_blocks[0, 0]
    )
    stages = lax.axis_size("pipe")
    stage = lax.axis_index("pipe").astype(jnp.int32)[None]
    front = (query_fwd[0], key_fwd[0], value_fwd[0])
    first = exchange(
        pack_first(stage, (query_bwd[0], key_bwd[0], value_bwd[0], grad_mix[0]), front)
    )
    lead, rest = pack_rest(front)
    received = lax.ppermute(lead, "pipe", outward(stages))
    parts, _, rows, _ = first.shape
    quarter, eighth = rows // QUARTERS, rows // EIGHTHS
    lent = jnp.concatenate([stage, QUARTERS - 1 - from_end(stage, stages)])
    second = merge(lent, quarter, [received], rest)
    second, ids, bias = lax.optimization_barrier((second, ids, bias))
    second = exchange(second)
    early, last, rest = attention(
        backward_kernel, 3, [rows - 2 * eighth, eighth, rows - eighth],
        stage, ids, bias, [first], [], [pltpu.VMEM((parts * rows, HDIM), jnp.float32)] * 2, 5,
    )
    early = passed_along(early, "pipe", -1)
    last = lax.ppermute(last, "pipe", [(1, 0)])
    lent = jnp.concatenate([stage, EIGHTHS - 1 - stage])
    grads = merge(lent, eighth, [early, last], rest)
    back = lax.ppermute(second, "pipe", [(b, a) for a, b in outward(stages)])
    (mixed,) = attention(
        forward_kernel, 1, [rows], stage, ids, bias, [], [first, second, back],
        [
            pltpu.VMEM((parts, 3, rows, HDIM), jnp.bfloat16),
            pltpu.SemaphoreType.DMA((QUARTERS,)),
        ],
        2,
    )
    mixed = passed_along(mixed, "pipe", 1)
    grads = exchange(grads)
    late = passed_along(grads, "pipe", -1)
    mixed = exchange(mixed)
    grads, mixed = unpack(lent, grads, late, mixed)
    return (mixed, grads[:, None])


def solution(mesh):
    rows = P("pipe", ("seq", "tp"), None, None)
    placed = (rows,) * 7 + (
        P("pipe", ("seq", "tp"), None),
        P("pipe", ("seq", "tp")),
        P("pipe", ("seq", "tp")),
        P("pipe", ("seq", "tp"), None, None),
    )
    return jax.shard_map(
        body,
        mesh=mesh,
        in_specs=placed,
        out_specs=(rows, P(None, "pipe", ("seq", "tp"), None, None)),
        check_vma=False,
    )
```

```python
import math

import jax
import jax.numpy as jnp
from jax import lax
from jax.experimental import pallas as pl
from jax.experimental.pallas import tpu as pltpu
from jax.sharding import PartitionSpec as P

BLK = 64
GLOBAL = 2
WMAX = 1
R_MOST = 3
SLOTS = 8
HDIM = 128
SCALE = HDIM ** (-0.5)
LOG2E = math.log2(math.e)
MIB = 1 << 20
STEP = 16
QUARTERS = 4
EIGHTHS = 8


def passed_along(value, axis, steps):
    count = lax.axis_size(axis)
    first, last = (max(0, -steps), min(count, count - steps))
    return lax.ppermute(value, axis, [(source, source + steps) for source in range(first, last)])


def key_slots(glob, win, count, rand_ids):
    nblk = rand_ids.shape[0]
    blocks = jnp.arange(nblk, dtype=jnp.int32)[:, None]
    glob_ids = jnp.broadcast_to(glob[None, :], (nblk, GLOBAL))
    glob_open = jnp.ones((nblk, GLOBAL), jnp.bool_)
    offsets = jnp.arange(-WMAX, WMAX + 1, dtype=jnp.int32)[None, :]
    near = blocks + offsets
    near_open = (jnp.abs(offsets) <= win) & (near >= 0) & (near < nblk)
    near = jnp.clip(near, 0, nblk - 1)
    rand_open = jnp.broadcast_to(
        jnp.arange(R_MOST, dtype=jnp.int32)[None, :] < count, (nblk, R_MOST)
    )
    ids = jnp.concatenate([glob_ids, near, rand_ids], axis=1)
    opened = jnp.concatenate([glob_open, near_open, rand_open], axis=1)
    same = ids[:, :, None] == ids[:, None, :]
    earlier = jnp.arange(SLOTS)[None, :] < jnp.arange(SLOTS)[:, None]
    repeated = jnp.any(same & opened[:, None, :] & earlier[None], axis=2)
    return (ids, opened & jnp.logical_not(repeated))


def pack_first_kernel(stage, *refs):
    back, front, out, (wide, heads, sem, out_sem) = refs[:4], refs[4:7], refs[7], refs[8:]
    rows = back[0].shape[0]
    chunks = sem.shape[1]
    size = rows // chunks

    def copy(x, a, c):
        at = pl.ds(c * size, size)
        return pltpu.make_async_copy(x.at[at], wide.at[a, at], sem.at[a, c])

    @pl.when(stage[0] != 0)
    def _():
        for c in range(chunks):
            for a in range(4):
                copy(back[a], a, c).start()

    @pl.when(stage[0] == 0)
    def _():
        for c in range(chunks):
            for a in range(4):
                copy(front[min(a, 2)], a, c).start()

    writes = []
    for c in range(chunks):
        at = pl.ds(c * size, size)
        for a in range(4):
            copy(back[a], a, c).wait()
            heads[:, a, c * size : (c + 1) * size] = jnp.swapaxes(
                wide[a, c * size : (c + 1) * size], 0, 1
            )
        writes.append(pltpu.make_async_copy(heads.at[:, :, at], out.at[:, :, at], out_sem.at[c]))
        writes[-1].start()
    for write in writes:
        write.wait()


def pack_first(stage, back, front):
    rows, heads, hdim = back[0].shape
    return pl.pallas_call(
        pack_first_kernel,
        in_specs=[pl.BlockSpec(memory_space=pltpu.SMEM)]
        + [pl.BlockSpec(memory_space=pl.ANY)] * 7,
        out_specs=pl.BlockSpec(memory_space=pl.ANY),
        out_shape=jax.ShapeDtypeStruct((heads, 4, rows, hdim), jnp.bfloat16),
        scratch_shapes=[
            pltpu.VMEM((4, rows, heads, hdim), jnp.bfloat16),
            pltpu.VMEM((heads, 4, rows, hdim), jnp.bfloat16),
            pltpu.SemaphoreType.DMA((4, 4)),
            pltpu.SemaphoreType.DMA((4,)),
        ],
        compiler_params=pltpu.CompilerParams(vmem_limit_bytes=60 * MIB),
        name="pack_first",
    )(stage, *back, *front)


def pack_rest_kernel(*refs):
    ins, lead, rest = refs[:-2], refs[-2], refs[-1]
    quarter = ins[0].shape[0] // QUARTERS
    for a, x in enumerate(ins):
        heads = jnp.swapaxes(x[...], 0, 1)
        lead[:, a] = heads[:, :-quarter]
        rest[:, a] = heads[:, quarter:]


def pack_rest(arrays):
    rows, heads, hdim = arrays[0].shape
    shape = (heads, len(arrays), rows - rows // QUARTERS, hdim)
    return pl.pallas_call(
        pack_rest_kernel,
        out_shape=[jax.ShapeDtypeStruct(shape, jnp.bfloat16)] * 2,
        compiler_params=pltpu.CompilerParams(vmem_limit_bytes=60 * MIB),
        cost_estimate=pl.CostEstimate(flops=0, bytes_accessed=9 * MIB, transcendentals=0),
        name="pack_rest",
    )(*arrays)


def from_end(stage, stages):
    return jnp.minimum(stage, stages - 1 - stage)


def merge_kernel(size, stage, *refs):
    received, rest, out = refs[:-2], refs[-2], refs[-1]
    f = 0
    for x in received:
        for n in range(x.shape[2] // size):
            to, at = slice(f * size, (f + 1) * size), slice(n * size, (n + 1) * size)

            @pl.when(f < stage[1])
            def _():
                out[:, :, to] = x[:, :, at]

            @pl.when(f >= stage[1])
            def _():
                out[:, :, to] = rest[:, :, to]

            f += 1


def merge(stage, size, received, rest):
    in_vmem = pl.BlockSpec(memory_space=pltpu.VMEM)
    return pl.pallas_call(
        lambda *refs: merge_kernel(size, *refs),
        in_specs=[pl.BlockSpec(memory_space=pltpu.SMEM)] + [in_vmem] * (len(received) + 1),
        out_shape=jax.ShapeDtypeStruct(rest.shape, rest.dtype),
        compiler_params=pltpu.CompilerParams(vmem_limit_bytes=40 * MIB),
        cost_estimate=pl.CostEstimate(flops=0, bytes_accessed=8 * MIB, transcendentals=0),
        name="merge",
    )(stage, *received, rest)


def unpack_kernel(stage, own, late, mixed, out, mixed_out, x, heads, mixed_heads, sem, out_sem):
    steps = out_sem.shape[0] - 1
    size = x.shape[2] // (EIGHTHS - 1)
    rows = heads.shape[1] // steps

    def copy(e):
        at = pl.ds(e * size, size)
        return pltpu.make_async_copy(own.at[:, :, at], x.at[:, :, at], sem.at[e])

    def put(ref, slot, e):
        for a in range(heads.shape[0]):
            heads[a, e * size : (e + 1) * size] = jnp.swapaxes(
                ref[:, a, slot * size : (slot + 1) * size], 0, 1
            )

    for e in range(EIGHTHS - 1):
        pl.when(e < stage[1])(copy(e).start)
    mixed_heads[...] = jnp.swapaxes(mixed[:, 0], 0, 1)
    writes = [pltpu.make_async_copy(mixed_heads, mixed_out.at[0], out_sem.at[steps])]
    writes[-1].start()
    for h in range(steps):
        for e in range(h * EIGHTHS // steps, (h + 1) * EIGHTHS // steps):
            if e < EIGHTHS - 1:

                @pl.when(e < stage[1])
                def _():
                    copy(e).wait()
                    put(x, e, e)

            @pl.when(e >= stage[1])
            def _():
                put(late, max(e - 1, 0), e)

        at = pl.ds(h * rows, rows)
        writes.append(pltpu.make_async_copy(heads.at[:, at], out.at[:, at], out_sem.at[h]))
        writes[-1].start()
    for write in writes:
        write.wait()


def unpack(stage, own, late, mixed):
    heads, count, some, hdim = own.shape
    rows = some * EIGHTHS // (EIGHTHS - 1)
    anywhere = pl.BlockSpec(memory_space=pl.ANY)
    in_vmem = pl.BlockSpec(memory_space=pltpu.VMEM)
    return pl.pallas_call(
        unpack_kernel,
        in_specs=[pl.BlockSpec(memory_space=pltpu.SMEM), anywhere, in_vmem, in_vmem],
        out_specs=[anywhere] * 2,
        out_shape=[
            jax.ShapeDtypeStruct((count, rows, heads, hdim), jnp.bfloat16),
            jax.ShapeDtypeStruct((1, rows, heads, hdim), jnp.bfloat16),
        ],
        scratch_shapes=[
            pltpu.VMEM((heads, count, some, hdim), jnp.bfloat16),
            pltpu.VMEM((count, rows, heads, hdim), jnp.bfloat16),
            pltpu.VMEM((rows, heads, hdim), jnp.bfloat16),
            pltpu.SemaphoreType.DMA((EIGHTHS - 1,)),
            pltpu.SemaphoreType.DMA((4 + 1,)),
        ],
        compiler_params=pltpu.CompilerParams(vmem_limit_bytes=32 * MIB),
        cost_estimate=pl.CostEstimate(flops=0, bytes_accessed=8 * MIB, transcendentals=0),
        name="unpack",
    )(stage, own, late, mixed)


def outward(stages):
    half = stages // 2
    return [(p, p - 1) for p in range(1, half)] + [(p, p + 1) for p in range(half, stages - 1)]


def dot(a, b, dims):
    return lax.dot_general(a, b, (dims, ((), ())), preferred_element_type=jnp.float32)


def block(ref, a, b):
    per = ref.shape[2] // BLK
    return ref[b // per, a, pl.ds(pl.multiple_of((b % per) * BLK, BLK), BLK), :]


def gather(x, a, picks):
    return jnp.concatenate([block(x, a, b) for b in picks], axis=0)


def probabilities(scores, bias):
    scores = [s * (SCALE * LOG2E) + b for s, b in zip(scores, bias)]
    weights = [jnp.exp2(s - jnp.max(s, axis=-1, keepdims=True)) for s in scores]
    return [w * (1.0 / jnp.sum(w, axis=-1, keepdims=True)) for w in weights]


def step_blocks(t, ids, x):
    per = x.shape[2] // BLK
    blocks = [t * STEP + n for n in range(STEP)]
    picks = [[ids[i, c] for c in range(SLOTS)] for i in blocks]
    places = [
        (t * (STEP // per) + n // per, slice((n % per) * BLK, (n % per + 1) * BLK))
        for n in range(STEP)
    ]
    return blocks, picks, places


def forward_kernel(stages, stage, ids, bias, whole, own, back, out, x, sem):
    edge = from_end(stage[0], stages)
    lent = QUARTERS - edge
    quarter = x.shape[2] // QUARTERS

    def copy(ref, f, e):
        return pltpu.make_async_copy(
            ref.at[:, pl.ds(0, x.shape[1]), pl.ds(f * quarter, quarter)],
            x.at[:, :, pl.ds(e * quarter, quarter)],
            sem.at[e],
        )

    for e in range(QUARTERS):
        pl.when(edge == 0)(copy(whole, e, e).start)
        if e < QUARTERS - 1:
            pl.when((edge > 0) & (e < lent))(copy(back, e, e).start)
        if e > 0:
            pl.when((edge > 0) & (e >= lent))(copy(own, e - 1, e).start)
    for e in range(QUARTERS):
        copy(whole, e, e).wait()

    def step(t, carry):
        blocks, picks, places = step_blocks(t, ids, x)
        keys = [gather(x, 1, p) for p in picks]
        values = [gather(x, 2, p) for p in picks]
        queries = [x[j, 0, own, :] for j, own in places]
        scores = [dot(q, k, ((1,), (1,))) for q, k in zip(queries, keys)]
        prob = probabilities(scores, [bias[pl.ds(i, 1), :] for i in blocks])
        prob = [p.astype(jnp.bfloat16) for p in prob]
        for (j, own), p, v in zip(places, prob, values):
            out[j, 0, own, :] = dot(p, v, ((1,), (0,))).astype(jnp.bfloat16)
        return carry

    lax.fori_loop(0, ids.shape[0] // STEP, step, 0)


def backward_kernel(stages, stage, ids, bias, x, lead, last, rest, dk, dv):
    del stages, stage
    parts, _, rows, hdim = x.shape
    size = rows // EIGHTHS
    ranges = [(lead, 0), (last, rows - 2 * size), (rest, size)]

    def put(j, a, at, rows_of):
        count = rows_of.shape[-2]
        for out, start in ranges:
            low, high = max(at, start), min(at + count, start + out.shape[2])
            if low < high:
                out[j, a, low - start : high - start, :] = rows_of[..., low - at : high - at, :]

    dk[...] = jnp.zeros_like(dk)
    dv[...] = jnp.zeros_like(dv)

    def step(t, carry):
        blocks, picks, places = step_blocks(t, ids, x)
        keys = [gather(x, 1, p) for p in picks]
        values = [gather(x, 2, p) for p in picks]
        queries = [x[j, 0, own, :] for j, own in places]
        grads = [x[j, 3, own, :] for j, own in places]
        scores = [dot(q, k, ((1,), (1,))) for q, k in zip(queries, keys)]
        dprob = [dot(g, v, ((1,), (1,))) for g, v in zip(grads, values)]
        prob = probabilities(scores, [bias[pl.ds(i, 1), :] for i in blocks])
        prob_b = [p.astype(jnp.bfloat16) for p in prob]
        value_part = [dot(p, g, ((0,), (0,))) for p, g in zip(prob_b, grads)]
        delta = [
            jnp.sum(p.astype(jnp.float32) * d, axis=-1, keepdims=True)
            for p, d in zip(prob_b, dprob)
        ]
        dscore = [
            (p * ((d - e) * SCALE)).astype(jnp.bfloat16) for p, d, e in zip(prob, dprob, delta)
        ]
        key_part = [dot(d, q, ((0,), (0,))) for d, q in zip(dscore, queries)]
        for (j, own), d, k in zip(places, dscore, keys):
            put(j, 0, own.start, dot(d, k, ((1,), (0,))).astype(jnp.bfloat16))
        for pick, kp, vp in zip(picks, key_part, value_part):
            for c, b in enumerate(pick):
                at = pl.ds(pl.multiple_of(b * BLK, BLK), BLK)
                dk[at, :] += kp[c * BLK : (c + 1) * BLK]
                dv[at, :] += vp[c * BLK : (c + 1) * BLK]
        return carry

    lax.fori_loop(0, ids.shape[0] // STEP, step, 0)
    put(slice(None), 1, 0, dk[...].reshape(parts, rows, hdim).astype(jnp.bfloat16))
    put(slice(None), 2, 0, dv[...].reshape(parts, rows, hdim).astype(jnp.bfloat16))


def attention(kernel, results, lengths, stage, ids, bias, ins, rest, scratch, matmuls):
    parts, _, rows, hdim = (*ins, *rest)[0].shape
    work = parts * rows * SLOTS * BLK * hdim * 2
    stages = lax.axis_size("pipe")
    in_smem = pl.BlockSpec(memory_space=pltpu.SMEM)
    in_vmem = pl.BlockSpec(memory_space=pltpu.VMEM)
    return pl.pallas_call(
        lambda *refs: kernel(stages, *refs),
        out_shape=[
            jax.ShapeDtypeStruct((parts, results, n, hdim), jnp.bfloat16) for n in lengths
        ],
        in_specs=[in_smem, in_smem, in_vmem]
        + [in_vmem] * len(ins)
        + [pl.BlockSpec(memory_space=pl.ANY)] * len(rest),
        scratch_shapes=scratch,
        compiler_params=pltpu.CompilerParams(vmem_limit_bytes=(40 if ins else 60) * MIB),
        cost_estimate=pl.CostEstimate(
            flops=4 * matmuls * work, bytes_accessed=8 * MIB, transcendentals=0
        ),
        name=kernel.__name__,
    )(stage, ids, bias, *ins, *rest)


def exchange(x):
    return lax.all_to_all(x, ("seq", "tp"), split_axis=0, concat_axis=0, tiled=True)


def slots_and_bias(glob, win, count, rand_ids):
    ids, opened = key_slots(glob, win, count, rand_ids)
    bias = jnp.where(jnp.repeat(opened, BLK, axis=1), 0.0, -1e30).astype(jnp.float32)
    return ids, bias


def body(
    query_fwd,
    key_fwd,
    value_fwd,
    query_bwd,
    key_bwd,
    value_bwd,
    grad_mix,
    global_blocks,
    window,
    rand_count,
    rand_blocks,
):
    ids, bias = slots_and_bias(
        global_blocks[0, 0], window[0, 0], rand_count[0, 0], rand_blocks[0, 0]
    )
    stages = lax.axis_size("pipe")
    stage = lax.axis_index("pipe").astype(jnp.int32)[None]
    front = (query_fwd[0], key_fwd[0], value_fwd[0])
    first = exchange(
        pack_first(stage, (query_bwd[0], key_bwd[0], value_bwd[0], grad_mix[0]), front)
    )
    lead, rest = pack_rest(front)
    received = lax.ppermute(lead, "pipe", outward(stages))
    parts, _, rows, _ = first.shape
    quarter, eighth = rows // QUARTERS, rows // EIGHTHS
    lent = jnp.concatenate([stage, QUARTERS - 1 - from_end(stage, stages)])
    second = merge(lent, quarter, [received], rest)
    second, ids, bias = lax.optimization_barrier((second, ids, bias))
    second = exchange(second)
    early, last, rest = attention(
        backward_kernel, 3, [rows - 2 * eighth, eighth, rows - eighth],
        stage, ids, bias, [first], [], [pltpu.VMEM((parts * rows, HDIM), jnp.float32)] * 2, 5,
    )
    early = passed_along(early, "pipe", -1)
    last = lax.ppermute(last, "pipe", [(1, 0)])
    lent = jnp.concatenate([stage, EIGHTHS - 1 - stage])
    grads = merge(lent, eighth, [early, last], rest)
    back = lax.ppermute(second, "pipe", [(b, a) for a, b in outward(stages)])
    (mixed,) = attention(
        forward_kernel, 1, [rows], stage, ids, bias, [], [first, second, back],
        [
            pltpu.VMEM((parts, 3, rows, HDIM), jnp.bfloat16),
            pltpu.SemaphoreType.DMA((QUARTERS,)),
        ],
        2,
    )
    mixed = passed_along(mixed, "pipe", 1)
    grads = exchange(grads)
    late = passed_along(grads, "pipe", -1)
    mixed = exchange(mixed)
    grads, mixed = unpack(lent, grads, late, mixed)
    return (mixed, grads[:, None])


def solution(mesh):
    rows = P("pipe", ("seq", "tp"), None, None)
    placed = (rows,) * 7 + (
        P("pipe", ("seq", "tp"), None),
        P("pipe", ("seq", "tp")),
        P("pipe", ("seq", "tp")),
        P("pipe", ("seq", "tp"), None, None),
    )
    return jax.shard_map(
        body,
        mesh=mesh,
        in_specs=placed,
        out_specs=(rows, P(None, "pipe", ("seq", "tp"), None, None)),
        check_vma=False,
    )
```
